256 devices in a mesh: sub: 16 (over y_lo, z), bl: 16 (over x, y_hi, core).
Axes of the slice: x: 4, y: 4 (y_hi: 2, y_lo: 2; y = y_hi * 2 + y_lo), z: 8, core: 2. Of those that a mesh axis runs over, the one named last changes fastest.
Arguments:
- coherency: bfloat16 [128, 32768, 128], P('sub', 'bl'), may hold values from -1.5 to 1.5
- visibility: float32 [2, 128, 32768], P(None, 'sub', 'bl'), may hold values from -24 to 24
- stations: int32 [2, 32768], P(None, 'bl'), may hold values from 0 to 511, as said below
- gains: float32 [128, 512, 128], P('sub', 'bl'), may hold values from -6 to 6
- dual: float32 [128, 512, 128], P('sub', 'bl'), may hold values from -3 to 3
- coeffs: float32 [4, 512, 128], P(None, 'bl'), may hold values from -6 to 6
- penalty: int32 [128], replicated, may hold values from 1 to 8
Outputs:
- new_gains: float32 [128, 512, 128], P('sub', 'bl')
- new_dual: float32 [128, 512, 128], P('sub', 'bl')
- new_coeffs: float32 [4, 512, 128], P(None, 'bl')
The draws below stay inside these ranges and needn't reach their ends.
Inputs may be any that keep to these rules, and one draw needn't show every extreme that they name: The two stations of every baseline differ.
All inputs are finite; a program needn't handle non-finite values.
Results may differ from the reference program's by a relative error of at most 0.0028.
Values sent between devices are 32-bit elements; how exact they have to be, the bound alone decides.
A program may use at most 128 MiB of HBM per device.

```python
import math
import jax
import jax.numpy as jnp
from jax import lax

STATION_TOTAL = 512
DIRECTION_COUNT = 64
P_SIZE = 4
CHANNEL_COUNT = 128
BASELINE_TOTAL = 32768


def draw_stations(key, part):
    key = jax.random.fold_in(key, 11)
    primary_key, secondary_key = jax.random.split(key)
    lower_edge = jax.random.randint(primary_key, (BASELINE_TOTAL,), 0, STATION_TOTAL, dtype=jnp.int32)
    shift_amount = jax.random.randint(secondary_key, (BASELINE_TOTAL,), 1, STATION_TOTAL, dtype=jnp.int32)
    return jnp.stack([lower_edge, (lower_edge + shift_amount) % STATION_TOTAL])


def touch_ends(entries, stream_key, low, top_value):
    spot = [jax.random.randint(jax.random.fold_in(stream_key, axis), (), 0, length) for axis, length in enumerate(entries.shape)]
    main_axis = entries.shape.index(max(entries.shape))
    beside = spot[:main_axis] + [(spot[main_axis] + 1) % entries.shape[main_axis]] + spot[main_axis + 1:]
    return entries.at[tuple(spot)].set(low).at[tuple(beside)].set(top_value)


def shard_levels(rng, extent, cuts, low, high):
    factor_of = 1.0
    for dim, parts in cuts:
        draws = jax.random.uniform(jax.random.fold_in(jax.random.fold_in(rng, 6), dim), (parts,), jnp.float32, low / len(cuts), high / len(cuts))
        factor_of = factor_of * jnp.repeat(jnp.exp(draws), extent[dim] // parts).reshape((-1,) + (1,) * (len(extent) - 1 - dim))
    return factor_of


def centred(rng, extent, deviation, most, pieces=(), kind=jnp.bfloat16):
    result = jax.random.normal(rng, extent, jnp.float32) * deviation
    if len(pieces) > 0:
        result = shard_levels(rng, extent, pieces, -0.22, 0.18) * result
    return jnp.clip(result, min=-most, max=most).astype(kind)


def setup_inputs(seed: int = 0) -> dict:
    keys = jax.random.split(jax.random.key(seed), 8)
    return {
        "coherency": centred(keys[0], (CHANNEL_COUNT, BASELINE_TOTAL, 2 * DIRECTION_COUNT), 0.25, 1.5, ((0, 16), (1, 16))),
        "visibility": centred(keys[1], (2, CHANNEL_COUNT, BASELINE_TOTAL), 4.0, 24.0, ((1, 16), (2, 16)), jnp.float32),
        "stations": draw_stations(jax.random.fold_in(keys[7], 71), 0),
        "gains": centred(keys[3], (CHANNEL_COUNT, STATION_TOTAL, 2 * DIRECTION_COUNT), 1.0, 6.0, ((0, 16), (1, 16)), jnp.float32),
        "dual": centred(keys[4], (CHANNEL_COUNT, STATION_TOTAL, 2 * DIRECTION_COUNT), 0.5, 3.0, ((0, 16), (1, 16)), jnp.float32),
        "coeffs": centred(keys[5], (P_SIZE, STATION_TOTAL, 2 * DIRECTION_COUNT), 1.0, 6.0, ((1, 16),), jnp.float32),
        "penalty": touch_ends(jax.random.randint(keys[6], (CHANNEL_COUNT,), 1, 9), jax.random.fold_in(keys[6], 1), 1, 8).astype(jnp.int32),
    }


def bernstein_table(count, terms):
    position = (jnp.arange(count).astype(jnp.float32) + 0.5) / count
    degree = terms - 1
    return jnp.stack([math.comb(degree, order) * position ** order * (1.0 - position) ** (degree - order) for order in range(terms)])

def channel_terms(coh, vis_re, vis_im, gain_table, lower_edge, right_end):
    half_width = gain_table.shape[-1] // 2
    near = jnp.take(gain_table, lower_edge, axis=-2)
    far = jnp.take(gain_table, right_end, axis=-2)
    near_re, near_im = (near[..., :half_width], near[..., half_width:])
    far_re, far_im = (far[..., :half_width], far[..., half_width:])
    coh_f = coh.astype(jnp.float32)
    coh_re, coh_im = (coh_f[..., :half_width], coh_f[..., half_width:])
    hat_re = coh_re * far_re + coh_im * far_im
    hat_im = coh_im * far_re - coh_re * far_im
    model_re = near_re * hat_re - near_im * hat_im
    model_im = near_re * hat_im + near_im * hat_re
    resid_re = vis_re - jnp.sum(model_re, axis=-1)
    resid_im = vis_im - jnp.sum(model_im, axis=-1)
    target_re = resid_re[..., None] + model_re
    target_im = resid_im[..., None] + model_im
    tilde_re = coh_re * near_re - coh_im * near_im
    tilde_im = coh_re * near_im + coh_im * near_re
    terms_left = jnp.concatenate([target_re * hat_re + target_im * hat_im, target_im * hat_re - target_re * hat_im, hat_re * hat_re + hat_im * hat_im], axis=-1)
    terms_right = jnp.concatenate([target_re * tilde_re + target_im * tilde_im, target_re * tilde_im - target_im * tilde_re, tilde_re * tilde_re + tilde_im * tilde_im], axis=-1)
    return (terms_left.astype(jnp.bfloat16), terms_right.astype(jnp.bfloat16))

def gain_update(normals, dual, prior, weights):
    width_two = dual.shape[-1]
    numerator = normals[..., :width_two]
    squares = normals[..., width_two:]
    denominator = jnp.concatenate([squares, squares], axis=-1) + weights[:, None, None]
    return (numerator + weights[:, None, None] * (prior - dual)) / denominator

def poly_solve(lower, moments):
    terms = moments.shape[0]
    forward = []
    for row in range(terms):
        value = moments[row]
        for col in range(row):
            value = value - lower[row, col] * forward[col]
        forward.append(value / lower[row, row])
    backward = [None] * terms
    for row in range(terms - 1, -1, -1):
        value = forward[row]
        for col in range(row + 1, terms):
            value = value - lower[col, row] * backward[col]
        backward[row] = value / lower[row, row]
    return jnp.stack(backward)

def reference(coherency, visibility, stations, gains, dual, coeffs, penalty):
    station_count = gains.shape[1]
    lower_edge = stations[0]
    right_end = stations[1]

    def per_channel(index):
        terms_left, terms_right = channel_terms(coherency[index], visibility[0, index], visibility[1, index], gains[index], lower_edge, right_end)
        terms_left = lax.optimization_barrier(terms_left).astype(jnp.float32)
        terms_right = lax.optimization_barrier(terms_right).astype(jnp.float32)
        return jax.ops.segment_sum(terms_left, lower_edge, num_segments=station_count) + jax.ops.segment_sum(terms_right, right_end, num_segments=station_count)
    normals = lax.map(per_channel, jnp.arange(CHANNEL_COUNT).astype(jnp.int32))
    bernstein = bernstein_table(CHANNEL_COUNT, P_SIZE)
    weights = 4.0 * penalty.astype(jnp.float32)
    prior = jnp.einsum('jf,jsc->fsc', bernstein, coeffs, precision=lax.Precision.HIGHEST)
    new_gains = gain_update(normals, dual, prior, weights)
    weighted = bernstein * weights[None, :]
    gram_matrix = jnp.dot(weighted, bernstein.T, precision=lax.Precision.HIGHEST)
    factor_lower = jnp.linalg.cholesky(gram_matrix)
    moments = jnp.einsum('jf,fsc->jsc', weighted, new_gains + dual, precision=lax.Precision.HIGHEST)
    new_coeffs = poly_solve(factor_lower, moments)
    consensus = jnp.einsum('jf,jsc->fsc', bernstein, new_coeffs, precision=lax.Precision.HIGHEST)
    new_dual = dual + new_gains - consensus
    return (new_gains, new_dual, new_coeffs)
```

```python
import functools
import math

import jax
import jax.numpy as jnp
from jax import lax
from jax.experimental import pallas as pl
from jax.experimental.pallas import tpu as pltpu
from jax.sharding import PartitionSpec as P

MESH = pl.DeviceIdType.MESH
BF = jnp.bfloat16
F32 = jnp.float32
PAIRS = 4
STATIONS = 512
HALF = 256
OWN = 32
BASE = 2048
CHIPS = 8
SUBS = 16
TERMS = 4
BLOCK = 512


def bernstein(position):
    degree = TERMS - 1
    rest = 1.0 - position
    out = []
    for order in range(TERMS):
        value = jnp.full_like(position, float(math.comb(degree, order)))
        for _ in range(order):
            value = value * position
        for _ in range(degree - order):
            value = value * rest
        out.append(value)
    return out


def swap_halves(value):
    return pltpu.roll(value, 64, 1)


def kernel(
    coh_hbm, vis_hbm, gains_ref, dual_ref, coeffs_ref, stations_ref, pen_row, pen_smem,
    ng_ref, nd_ref, nc_ref,
    coh, vis, wide, cols, colb, hot_p, hot_q, hot_pt, hot_qt, mix,
    table, split, terms_p, terms_q, sums, core_in, chip_sum, chip_in,
    mom, mom_in, mom_all, fac,
    load_sem, ag_send, ag_recv, relay_send, relay_recv, core_send, core_recv,
    rs_send, rs_recv, m_send, m_recv, r_send, r_recv,
):
    k = lax.axis_index("sub")
    i = lax.axis_index("bl")
    m = i // 2
    c = i % 2
    other = (k, m * 2 + (1 - c))

    def chip_peer(d):
        return (k, lax.rem(m + d, CHIPS) * 2 + c)

    def sub_peer(d):
        return (lax.rem(k + d, SUBS), i)

    load_vis = pltpu.make_async_copy(vis_hbm, vis, load_sem.at[0])
    load_vis.start()
    load_coh = pltpu.make_async_copy(coh_hbm, coh, load_sem.at[1])
    load_coh.start()

    barrier = pltpu.get_barrier_semaphore()
    pl.semaphore_signal(barrier, inc=1, device_id=other, device_id_type=MESH)
    for d in range(1, CHIPS):
        pl.semaphore_signal(barrier, inc=1, device_id=chip_peer(d), device_id_type=MESH)
    for d in range(1, SUBS):
        pl.semaphore_signal(barrier, inc=1, device_id=sub_peer(d), device_id_type=MESH)

    low = lax.broadcasted_iota(jnp.int32, (OWN, 128), 1) < 64
    own_row = pl.multiple_of(c * HALF + m * OWN, OWN)
    for j in range(PAIRS):
        first, second = gains_ref[2 * j], gains_ref[2 * j + 1]
        table[j, pl.ds(own_row, OWN), 0:128] = jnp.where(low, first, swap_halves(second))
        table[j, pl.ds(own_row, OWN), 128:256] = jnp.where(low, swap_halves(first), second)

    pl.semaphore_wait(barrier, 1 + (CHIPS - 1) + (SUBS - 1))

    for j in range(PAIRS):
        for d in range(1, CHIPS):
            rows = table.at[j, pl.ds(own_row, OWN)]
            pltpu.make_async_remote_copy(
                src_ref=rows, dst_ref=rows, send_sem=ag_send.at[j], recv_sem=ag_recv.at[j],
                device_id=chip_peer(d), device_id_type=MESH,
            ).start()

    raw = stations_ref[...]
    spot = ((raw >> 5) & 1) * HALF + (raw >> 6) * OWN + (raw & 31)
    load_vis.wait()
    spot_f = spot.astype(F32)
    seen = vis[...].reshape(16, BASE)
    coarse = seen.astype(BF).astype(F32)
    wide[...] = jnp.zeros_like(wide)
    wide[0:16] = coarse
    wide[16:32] = seen - coarse
    wide[32:34] = spot_f

    def turn(t, _):
        at = pl.ds(pl.multiple_of(t * 128, 128), 128)
        piece = wide[:, at].T
        cols[at, :] = piece
        colb[at, :] = piece.astype(BF)
        for hot, col in ((hot_p, 32), (hot_q, 33)):
            lane = lax.broadcasted_iota(jnp.int32, (128, STATIONS), 1).astype(F32)
            hot[at, :] = jnp.where(piece[:, col:col + 1] == lane, 1.0, 0.0).astype(BF)
        return 0

    lax.fori_loop(0, BASE // 128, turn, 0)

    def turn_t(t, _):
        at = pl.ds(pl.multiple_of(t * 32, 32), 32)
        row = (lax.broadcasted_iota(jnp.int32, (32, BASE), 0) + t * 32).astype(F32)
        hot_pt[at, :] = jnp.where(wide[32:33, :] == row, 1.0, 0.0).astype(BF)
        hot_qt[at, :] = jnp.where(wide[33:34, :] == row, 1.0, 0.0).astype(BF)
        return 0

    lax.fori_loop(0, STATIONS // 32, turn_t, 0)

    out_lane = lax.broadcasted_iota(jnp.int32, (128, 256), 1)
    in_row = lax.broadcasted_iota(jnp.int32, (128, 256), 0)
    in_lane = lax.broadcasted_iota(jnp.int32, (256, 256), 0)
    out_wide = lax.broadcasted_iota(jnp.int32, (256, 256), 1)
    for j in range(PAIRS):
        want = (out_lane // 128) * 8 + 2 * j + (out_lane // 64) % 2
        hit = (in_row < 32) & (in_row % 16 == want)
        minus = jnp.where(in_lane // 64 == out_wide // 64, -1.0, 0.0).astype(BF)
        mix[j, 0:256] = minus
        mix[j, 256:512] = minus
        mix[j, 512:640] = jnp.where(hit, 1.0, 0.0).astype(BF)

    channel = lax.broadcasted_iota(jnp.int32, (1, 128), 1).astype(F32)
    rows_b = bernstein((channel + 0.5) / 128.0)
    weight_row = 4.0 * pen_row[...].astype(F32)
    lower = {}
    for r in range(TERMS):
        for q in range(r + 1):
            value = jnp.sum(weight_row * rows_b[r] * rows_b[q], axis=1, keepdims=True)
            for s in range(q):
                value = value - lower[r, s] * lower[q, s]
            lower[r, q] = jnp.sqrt(value) if r == q else value / lower[q, q]
            fac[4 * r + q:4 * r + q + 1, :] = jnp.broadcast_to(lower[r, q], (1, 128))

    load_coh.wait()

    def relay(j):
        got = table.at[j, pl.ds(0, (CHIPS - 1) * OWN)]
        pltpu.make_async_remote_copy(
            src_ref=got, dst_ref=got, send_sem=ag_send.at[j], recv_sem=ag_recv.at[j],
            device_id=other, device_id_type=MESH,
        ).wait_recv()
        half = table.at[j, pl.ds(pl.multiple_of(c * HALF, HALF), HALF)]
        pltpu.make_async_remote_copy(
            src_ref=half, dst_ref=half, send_sem=relay_send.at[j], recv_sem=relay_recv.at[j],
            device_id=other, device_id_type=MESH,
        ).start()

    def relay_copy(j):
        half = table.at[j, pl.ds(pl.multiple_of(c * HALF, HALF), HALF)]
        return pltpu.make_async_remote_copy(
            src_ref=half, dst_ref=half, send_sem=relay_send.at[j], recv_sem=relay_recv.at[j],
            device_id=other, device_id_type=MESH,
        )

    def core_copy(j):
        return pltpu.make_async_remote_copy(
            src_ref=sums.at[j, pl.ds(pl.multiple_of((1 - c) * HALF, HALF), HALF)],
            dst_ref=core_in.at[j], send_sem=core_send.at[j], recv_sem=core_recv.at[j],
            device_id=other, device_id_type=MESH,
        )

    def to_owners(j):
        core_copy(j).wait_recv()
        chip_sum[j] = sums[j, pl.ds(pl.multiple_of(c * HALF, HALF), HALF)] + core_in[j]
        for d in range(1, CHIPS):
            owner = lax.rem(m + d, CHIPS)
            pltpu.make_async_remote_copy(
                src_ref=chip_sum.at[j, pl.ds(pl.multiple_of(owner * OWN, OWN), OWN)],
                dst_ref=chip_in.at[j, d - 1], send_sem=rs_send.at[j], recv_sem=rs_recv.at[j],
                device_id=chip_peer(d), device_id_type=MESH,
            ).start()

    def all_in(j):
        return pltpu.make_async_remote_copy(
            src_ref=chip_in.at[j], dst_ref=chip_in.at[j], send_sem=rs_send.at[j],
            recv_sem=rs_recv.at[j], device_id=other, device_id_type=MESH,
        )

    wide_low = lax.broadcasted_iota(jnp.int32, (BLOCK, 128), 1) < 64

    relay(0)
    for j in range(PAIRS):
        relay_copy(j).wait_recv()
        whole = table[j]
        high = whole.astype(BF)
        split[0:512] = high
        split[512:1024] = (whole - high.astype(F32)).astype(BF)

        def block(b, _, j=j):
            at = pl.ds(pl.multiple_of(b * BLOCK, BLOCK), BLOCK)
            hp = hot_p[at, :]
            hq = hot_q[at, :]
            near = jnp.dot(jnp.concatenate([hp, hp], 1), split[...], preferred_element_type=F32)
            far = jnp.dot(jnp.concatenate([hq, hq], 1), split[...], preferred_element_type=F32)
            c0 = coh[2 * j, at, :].astype(F32)
            c1 = coh[2 * j + 1, at, :].astype(F32)
            cr = jnp.where(wide_low, c0, swap_halves(c1))
            ci = jnp.where(wide_low, swap_halves(c0), c1)
            nr, ni = near[:, 0:128], near[:, 128:256]
            fr, fi = far[:, 0:128], far[:, 128:256]
            hr = cr * fr + ci * fi
            hi = ci * fr - cr * fi
            mr = nr * hr - ni * hi
            mi = nr * hi + ni * hr
            mrh, mih = mr.astype(BF), mi.astype(BF)
            mrl = (mr - mrh.astype(F32)).astype(BF)
            mil = (mi - mih.astype(F32)).astype(BF)
            resid = jnp.dot(
                jnp.concatenate([mrh, mih, mrl, mil, colb[at, :]], 1), mix[j],
                preferred_element_type=F32,
            )
            tr = resid[:, 0:128] + mr
            ti = resid[:, 128:256] + mi
            er = cr * nr - ci * ni
            ei = cr * ni + ci * nr
            terms_p[at, 0:128] = (tr * hr + ti * hi).astype(BF)
            terms_p[at, 128:256] = (ti * hr - tr * hi).astype(BF)
            terms_p[at, 256:384] = (hr * hr + hi * hi).astype(BF)
            terms_q[at, 0:128] = (tr * er + ti * ei).astype(BF)
            terms_q[at, 128:256] = (tr * ei - ti * er).astype(BF)
            terms_q[at, 256:384] = (er * er + ei * ei).astype(BF)
            return 0

        lax.fori_loop(0, BASE // BLOCK, block, 0)
        if j + 1 < PAIRS:
            relay(j + 1)
        if j > 0:
            to_owners(j - 1)

        def scatter(r, _, j=j):
            at = pl.ds(pl.multiple_of(r * 256, 256), 256)
            sums[j, at, :] = jnp.dot(
                hot_pt[at, :], terms_p[...], preferred_element_type=F32
            ) + jnp.dot(hot_qt[at, :], terms_q[...], preferred_element_type=F32)
            return 0

        lax.fori_loop(0, STATIONS // 256, scatter, 0)
        core_copy(j).start()
    to_owners(PAIRS - 1)

    co = [coeffs_ref[t] for t in range(TERMS)]
    co_re = [jnp.where(low, v, swap_halves(v)) for v in co]
    co_im = [jnp.where(low, swap_halves(v), v) for v in co]
    half_lane = lax.broadcasted_iota(jnp.int32, (1, 128), 1)
    total = [jnp.zeros((OWN, 128), F32) for _ in range(TERMS)]
    basis_of = []
    for j in range(PAIRS):
        all_in(j).wait_recv()
        normal = chip_sum[j, pl.ds(pl.multiple_of(m * OWN, OWN), OWN)]
        for d in range(CHIPS - 1):
            normal = normal + chip_in[j, d]
        f0 = k * 8 + 2 * j
        p0 = jnp.full((1, 128), pen_smem[f0], jnp.int32)
        p1 = jnp.full((1, 128), pen_smem[f0 + 1], jnp.int32)
        w0 = 4.0 * p0.astype(F32)
        w1 = 4.0 * p1.astype(F32)
        spot0 = (jnp.full((1, 128), f0, jnp.int32).astype(F32) + 0.5) / 128.0
        spot1 = (jnp.full((1, 128), f0 + 1, jnp.int32).astype(F32) + 0.5) / 128.0
        b0, b1 = bernstein(spot0), bernstein(spot1)
        basis_of += [b0, b1]
        weight = jnp.where(half_lane < 64, w0, w1)
        both = [jnp.where(half_lane < 64, u, v) for u, v in zip(b0, b1)]
        d0, d1 = dual_ref[2 * j], dual_ref[2 * j + 1]
        dual_re = jnp.where(low, d0, swap_halves(d1))
        dual_im = jnp.where(low, swap_halves(d0), d1)
        prior_re = sum(both[t] * co_re[t] for t in range(TERMS))
        prior_im = sum(both[t] * co_im[t] for t in range(TERMS))
        below = normal[:, 256:384] + weight
        gain_re = (normal[:, 0:128] + weight * (prior_re - dual_re)) / below
        gain_im = (normal[:, 128:256] + weight * (prior_im - dual_im)) / below
        g0 = jnp.where(low, gain_re, swap_halves(gain_im))
        g1 = jnp.where(low, swap_halves(gain_re), gain_im)
        ng_ref[2 * j] = g0
        ng_ref[2 * j + 1] = g1
        for t in range(TERMS):
            total[t] = total[t] + (w0 * b0[t]) * (g0 + d0) + (w1 * b1[t]) * (g1 + d1)

    for t in range(TERMS):
        mom[4 * t:4 * t + 4] = total[t].reshape(4, 8, 128)
    for d in range(1, SUBS):
        pltpu.make_async_remote_copy(
            src_ref=mom.at[lax.rem(k + d, SUBS)], dst_ref=mom_in.at[d - 1],
            send_sem=m_send, recv_sem=m_recv, device_id=sub_peer(d), device_id_type=MESH,
        ).start()
    m_all = pltpu.make_async_remote_copy(
        src_ref=mom_in, dst_ref=mom_in, send_sem=m_send, recv_sem=m_recv,
        device_id=other, device_id_type=MESH,
    )
    m_all.wait_recv()
    tile = mom[k]
    for d in range(SUBS - 1):
        tile = tile + mom_in[d]
    mom_all[k] = tile
    for d in range(1, SUBS):
        pltpu.make_async_remote_copy(
            src_ref=mom_all.at[k], dst_ref=mom_all.at[k],
            send_sem=r_send, recv_sem=r_recv, device_id=sub_peer(d), device_id_type=MESH,
        ).start()
    r_all = pltpu.make_async_remote_copy(
        src_ref=mom_all.at[pl.ds(0, SUBS - 1)], dst_ref=mom_all.at[pl.ds(0, SUBS - 1)],
        send_sem=r_send, recv_sem=r_recv, device_id=other, device_id_type=MESH,
    )
    r_all.wait_recv()

    low_of = lambda r, q: fac[4 * r + q:4 * r + q + 1, :]
    forward = []
    for r in range(TERMS):
        value = mom_all[4 * r:4 * r + 4].reshape(OWN, 128)
        for q in range(r):
            value = value - low_of(r, q) * forward[q]
        forward.append(value / low_of(r, r))
    back = [None] * TERMS
    for r in range(TERMS - 1, -1, -1):
        value = forward[r]
        for q in range(r + 1, TERMS):
            value = value - low_of(q, r) * back[q]
        back[r] = value / low_of(r, r)
        nc_ref[r] = back[r]
    for f in range(2 * PAIRS):
        agreed = sum(basis_of[f][t] * back[t] for t in range(TERMS))
        nd_ref[f] = dual_ref[f] + ng_ref[f] - agreed

    for j in range(PAIRS):
        sent = table.at[j, pl.ds(0, (CHIPS - 1) * OWN)]
        pltpu.make_async_remote_copy(
            src_ref=sent, dst_ref=sent, send_sem=ag_send.at[j], recv_sem=ag_recv.at[j],
            device_id=other, device_id_type=MESH,
        ).wait_send()
        relay_copy(j).wait_send()
        core_copy(j).wait_send()
        all_in(j).wait_send()
    m_all.wait_send()
    r_all.wait_send()


def step(coherency, visibility, stations, gains, dual, coeffs, penalty):
    vmem = pl.BlockSpec(memory_space=pltpu.VMEM)
    hbm = pl.BlockSpec(memory_space=pl.ANY)
    dma = pltpu.SemaphoreType.DMA
    return pl.pallas_call(
        kernel,
        out_shape=(
            jax.ShapeDtypeStruct(gains.shape, F32),
            jax.ShapeDtypeStruct(gains.shape, F32),
            jax.ShapeDtypeStruct(coeffs.shape, F32),
        ),
        in_specs=[hbm, hbm, vmem, vmem, vmem, vmem, vmem, pl.BlockSpec(memory_space=pltpu.SMEM)],
        out_specs=(vmem, vmem, vmem),
        scratch_shapes=[
            pltpu.VMEM((8, BASE, 128), BF),
            pltpu.VMEM((2, 8, BASE), F32),
            pltpu.VMEM((128, BASE), F32),
            pltpu.VMEM((BASE, 128), F32),
            pltpu.VMEM((BASE, 128), BF),
            pltpu.VMEM((BASE, STATIONS), BF),
            pltpu.VMEM((BASE, STATIONS), BF),
            pltpu.VMEM((STATIONS, BASE), BF),
            pltpu.VMEM((STATIONS, BASE), BF),
            pltpu.VMEM((PAIRS, 640, 256), BF),
            pltpu.VMEM((PAIRS, STATIONS, 256), F32),
            pltpu.VMEM((2 * STATIONS, 256), BF),
            pltpu.VMEM((BASE, 384), BF),
            pltpu.VMEM((BASE, 384), BF),
            pltpu.VMEM((PAIRS, STATIONS, 384), F32),
            pltpu.VMEM((PAIRS, HALF, 384), F32),
            pltpu.VMEM((PAIRS, HALF, 384), F32),
            pltpu.VMEM((PAIRS, CHIPS - 1, OWN, 384), F32),
            pltpu.VMEM((SUBS, 8, 128), F32),
            pltpu.VMEM((SUBS - 1, 8, 128), F32),
            pltpu.VMEM((SUBS, 8, 128), F32),
            pltpu.VMEM((16, 128), F32),
            dma((2,)),
            dma((PAIRS,)), dma((PAIRS,)),
            dma((PAIRS,)), dma((PAIRS,)),
            dma((PAIRS,)), dma((PAIRS,)),
            dma((PAIRS,)), dma((PAIRS,)),
            dma(()), dma(()), dma(()), dma(()),
        ],
        compiler_params=pltpu.CompilerParams(
            collective_id=0, has_side_effects=True, vmem_limit_bytes=56 * 1024 * 1024
        ),
    )(coherency, visibility, gains, dual, coeffs, stations, penalty.reshape(1, 128), penalty)


def solution(mesh):
    placed = (
        P("sub", "bl", None),
        P(None, "sub", "bl"),
        P(None, "bl"),
        P("sub", "bl", None),
        P("sub", "bl", None),
        P(None, "bl", None),
        P(),
    )
    return jax.shard_map(
        step,
        mesh=mesh,
        in_specs=placed,
        out_specs=(P("sub", "bl", None), P("sub", "bl", None), P(None, "bl", None)),
        check_vma=False,
    )
```

```python
import functools
import math

import jax
import jax.numpy as jnp
from jax import lax
from jax.experimental import pallas as pl
from jax.experimental.pallas import tpu as pltpu
from jax.sharding import PartitionSpec as P

MESH = pl.DeviceIdType.MESH
BF = jnp.bfloat16
F32 = jnp.float32
PAIRS = 4
STATIONS = 512
HALF = 256
OWN = 32
BASE = 2048
CHIPS = 8
SUBS = 16
TERMS = 4
BLOCK = 512
CHIP_HOPS = ((2, 1), (2, 0), (1, 1), (3, 1), (0, 1), (1, 0), (3, 0))
SUB_HOPS = (
    (1, 4), (0, 4), (1, 3), (1, 5), (0, 3), (0, 5), (1, 2), (1, 6),
    (0, 2), (0, 6), (1, 1), (1, 7), (0, 1), (0, 7), (1, 0),
)


def bernstein(position):
    degree = TERMS - 1
    rest = 1.0 - position
    out = []
    for order in range(TERMS):
        value = jnp.full_like(position, float(math.comb(degree, order)))
        for _ in range(order):
            value = value * position
        for _ in range(degree - order):
            value = value * rest
        out.append(value)
    return out


def swap_halves(value):
    return pltpu.roll(value, 64, 1)


def kernel(
    coh_hbm, vis_hbm, gains_hbm, dual_hbm, coeffs_hbm, stations_hbm, pen_row, pen_smem,
    ng_hbm, mom_hbm, fac_hbm,
    coh, vis, gains_ref, dual_ref, coeffs_ref, stations_ref, ng_ref,
    wide, colb, hot, hot_pt, hot_qt, mix,
    table, split, pulled0, pulled1, terms_p, terms_q, sums, core_in, chip_sum, chip_in,
    mom, mom_in, mom_all, fac,
    ready, load_sem, out_sem, ag_send, ag_recv, relay_send, relay_recv, core_send, core_recv,
    rs_send, rs_recv, m_send, m_recv, r_send, r_recv,
):
    k = lax.axis_index("sub")
    i = lax.axis_index("bl")
    m = i // 2
    c = i % 2
    other = (k, m * 2 + (1 - c))

    def chip_at(hop):
        return lax.rem(m // 2 + hop[0], 4) * 2 + lax.rem(m + hop[1], 2)

    def chip_peer(hop):
        return (k, chip_at(hop) * 2 + c)

    def sub_at(hop):
        return lax.rem(k // 8 + hop[0], 2) * 8 + lax.rem(k + hop[1], 8)

    def sub_peer(hop):
        return (sub_at(hop), i)

    barrier = pltpu.get_barrier_semaphore()
    pl.semaphore_signal(barrier, inc=1, device_id=other, device_id_type=MESH)
    for hop in CHIP_HOPS:
        pl.semaphore_signal(barrier, inc=1, device_id=chip_peer(hop), device_id_type=MESH)
    above, below = sub_peer((0, 1)), sub_peer((0, 7))
    for near in (above, below, sub_peer((1, 0))):
        pl.semaphore_signal(barrier, inc=1, device_id=near, device_id_type=MESH)

    load_gains = pltpu.make_async_copy(gains_hbm, gains_ref, load_sem.at[2])
    load_gains.start()
    load_stations = pltpu.make_async_copy(stations_hbm, stations_ref, load_sem.at[3])
    load_stations.start()
    load_vis = pltpu.make_async_copy(vis_hbm, vis, load_sem.at[0])
    load_vis.start()
    load_coh = pltpu.make_async_copy(coh_hbm, coh, load_sem.at[1])
    load_coh.start()
    load_dual = pltpu.make_async_copy(dual_hbm, dual_ref, load_sem.at[4])
    load_dual.start()
    load_coeffs = pltpu.make_async_copy(coeffs_hbm, coeffs_ref, load_sem.at[5])
    load_coeffs.start()

    low = lax.broadcasted_iota(jnp.int32, (OWN, 128), 1) < 64
    load_gains.wait()
    own_row = pl.multiple_of(c * HALF + m * OWN, OWN)
    for j in range(PAIRS):
        first, second = gains_ref[2 * j], gains_ref[2 * j + 1]
        table[j, pl.ds(own_row, OWN), 0:128] = jnp.where(low, first, swap_halves(second))
        table[j, pl.ds(own_row, OWN), 128:256] = jnp.where(low, swap_halves(first), second)

    pl.semaphore_wait(barrier, 1 + (CHIPS - 1) + 3)

    def spread(j):
        for hop in CHIP_HOPS:
            rows = table.at[j, pl.ds(own_row, OWN)]
            pltpu.make_async_remote_copy(
                src_ref=rows, dst_ref=rows, send_sem=ag_send.at[j], recv_sem=ag_recv.at[j],
                device_id=chip_peer(hop), device_id_type=MESH,
            ).start()

    def heard(j):
        for near in (above, below):
            pl.semaphore_signal(ready.at[j], inc=1, device_id=near, device_id_type=MESH)

    spread(0)
    heard(0)

    load_stations.wait()
    raw = stations_ref[...]
    spot = ((raw >> 5) & 1) * HALF + (raw >> 6) * OWN + (raw & 31)
    load_vis.wait()
    spot_f = spot.astype(F32)
    seen = vis[...].reshape(16, BASE)
    coarse = seen.astype(BF).astype(F32)
    wide[...] = jnp.zeros_like(wide)
    wide[0:16] = coarse
    wide[16:32] = seen - coarse
    wide[32:34] = spot_f

    def turn(t, _):
        at = pl.ds(pl.multiple_of(t * 128, 128), 128)
        piece = wide[:, at].T
        colb[at, :] = piece.astype(BF)
        lane = lax.broadcasted_iota(jnp.int32, (128, STATIONS), 1).astype(F32)
        per = BLOCK // 128
        for end in range(2):
            to = pl.ds(pl.multiple_of(((t // per) * 2 + end) * BLOCK + (t % per) * 128, 128), 128)
            hot[to, :] = jnp.where(piece[:, 32 + end:33 + end] == lane, 1.0, 0.0).astype(BF)
        return 0

    lax.fori_loop(0, BASE // 128, turn, 0)

    def turn_t(t, _):
        at = pl.ds(pl.multiple_of(t * 32, 32), 32)
        row = (lax.broadcasted_iota(jnp.int32, (32, BASE), 0) + t * 32).astype(F32)
        hot_pt[at, :] = jnp.where(wide[32:33, :] == row, 1.0, 0.0).astype(BF)
        hot_qt[at, :] = jnp.where(wide[33:34, :] == row, 1.0, 0.0).astype(BF)
        return 0

    lax.fori_loop(0, STATIONS // 32, turn_t, 0)

    spread(1)
    out_lane = lax.broadcasted_iota(jnp.int32, (128, 256), 1)
    in_row = lax.broadcasted_iota(jnp.int32, (128, 256), 0)
    in_lane = lax.broadcasted_iota(jnp.int32, (256, 256), 0)
    out_wide = lax.broadcasted_iota(jnp.int32, (256, 256), 1)
    for j in range(PAIRS):
        want = (out_lane // 128) * 8 + 2 * j + (out_lane // 64) % 2
        hit = (in_row < 32) & (in_row % 16 == want)
        minus = jnp.where(in_lane // 64 == out_wide // 64, -1.0, 0.0).astype(BF)
        mix[j, 0:256] = minus
        mix[j, 256:512] = minus
        mix[j, 512:640] = jnp.where(hit, 1.0, 0.0).astype(BF)

    channel = lax.broadcasted_iota(jnp.int32, (1, 128), 1).astype(F32)
    rows_b = bernstein((channel + 0.5) / 128.0)
    weight_row = 4.0 * pen_row[...].astype(F32)
    lower = {}
    for r in range(TERMS):
        for q in range(r + 1):
            value = jnp.sum(weight_row * rows_b[r] * rows_b[q], axis=1, keepdims=True)
            for s in range(q):
                value = value - lower[r, s] * lower[q, s]
            lower[r, q] = jnp.sqrt(value) if r == q else value / lower[q, q]
            fac[4 * r + q:4 * r + q + 1, :] = jnp.broadcast_to(lower[r, q], (1, 128))

    load_coh.wait()

    def relay(j):
        got = table.at[j, pl.ds(0, (CHIPS - 1) * OWN)]
        pltpu.make_async_remote_copy(
            src_ref=got, dst_ref=got, send_sem=ag_send.at[j], recv_sem=ag_recv.at[j],
            device_id=other, device_id_type=MESH,
        ).wait_recv()
        half = table.at[j, pl.ds(pl.multiple_of(c * HALF, HALF), HALF)]
        pltpu.make_async_remote_copy(
            src_ref=half, dst_ref=half, send_sem=relay_send.at[j], recv_sem=relay_recv.at[j],
            device_id=other, device_id_type=MESH,
        ).start()

    def relay_copy(j):
        half = table.at[j, pl.ds(pl.multiple_of(c * HALF, HALF), HALF)]
        return pltpu.make_async_remote_copy(
            src_ref=half, dst_ref=half, send_sem=relay_send.at[j], recv_sem=relay_recv.at[j],
            device_id=other, device_id_type=MESH,
        )

    def core_copy(j):
        return pltpu.make_async_remote_copy(
            src_ref=sums.at[j, pl.ds(pl.multiple_of((1 - c) * HALF, HALF), HALF)],
            dst_ref=core_in.at[j], send_sem=core_send.at[j], recv_sem=core_recv.at[j],
            device_id=other, device_id_type=MESH,
        )

    def to_owners(j):
        core_copy(j).wait_recv()
        chip_sum[j] = sums[j, pl.ds(pl.multiple_of(c * HALF, HALF), HALF)] + core_in[j]
        for slot, hop in enumerate(CHIP_HOPS):
            owner = chip_at(hop)
            pltpu.make_async_remote_copy(
                src_ref=chip_sum.at[j, pl.ds(pl.multiple_of(owner * OWN, OWN), OWN)],
                dst_ref=chip_in.at[j, slot], send_sem=rs_send.at[j], recv_sem=rs_recv.at[j],
                device_id=chip_peer(hop), device_id_type=MESH,
            ).start()

    def all_in(j):
        return pltpu.make_async_remote_copy(
            src_ref=chip_in.at[j], dst_ref=chip_in.at[j], send_sem=rs_send.at[j],
            recv_sem=rs_recv.at[j], device_id=other, device_id_type=MESH,
        )

    wide_low = lax.broadcasted_iota(jnp.int32, (BLOCK, 128), 1) < 64

    relay(0)
    spread(2)

    def gather(b, pulled):
        both = hot[b * 2 * BLOCK:(b + 1) * 2 * BLOCK, :]
        pulled[...] = jnp.dot(
            jnp.concatenate([both, both], 1), split[...], preferred_element_type=F32
        )

    def combine(j, b, pulled):
        at = slice(b * BLOCK, (b + 1) * BLOCK)
        c0 = coh[2 * j, at, :].astype(F32)
        c1 = coh[2 * j + 1, at, :].astype(F32)
        cr = jnp.where(wide_low, c0, swap_halves(c1))
        ci = jnp.where(wide_low, swap_halves(c0), c1)
        nr, ni = pulled[0:BLOCK, 0:128], pulled[0:BLOCK, 128:256]
        fr, fi = pulled[BLOCK:2 * BLOCK, 0:128], pulled[BLOCK:2 * BLOCK, 128:256]
        hr = cr * fr + ci * fi
        hi = ci * fr - cr * fi
        mr = nr * hr - ni * hi
        mi = nr * hi + ni * hr
        mrh, mih = mr.astype(BF), mi.astype(BF)
        mrl = (mr - mrh.astype(F32)).astype(BF)
        mil = (mi - mih.astype(F32)).astype(BF)
        resid = jnp.dot(
            jnp.concatenate([mrh, mih, mrl, mil, colb[at, :]], 1), mix[j],
            preferred_element_type=F32,
        )
        tr = resid[:, 0:128] + mr
        ti = resid[:, 128:256] + mi
        er = cr * nr - ci * ni
        ei = cr * ni + ci * nr
        terms_p[at, 0:128] = (tr * hr + ti * hi).astype(BF)
        terms_p[at, 128:256] = (ti * hr - tr * hi).astype(BF)
        terms_p[at, 256:384] = (hr * hr + hi * hi).astype(BF)
        terms_q[at, 0:128] = (tr * er + ti * ei).astype(BF)
        terms_q[at, 128:256] = (tr * ei - ti * er).astype(BF)
        terms_q[at, 256:384] = (er * er + ei * ei).astype(BF)

    def scatter(rows, at):
        return jnp.dot(
            hot_pt[rows, at], terms_p[at, :], preferred_element_type=F32
        ) + jnp.dot(hot_qt[rows, at], terms_q[at, :], preferred_element_type=F32)

    blocks = BASE // BLOCK
    early = slice(0, BASE - BLOCK)
    late = slice(BASE - BLOCK, BASE)
    theirs = pl.ds(pl.multiple_of((1 - c) * HALF, HALF), HALF)
    mine = pl.ds(pl.multiple_of(c * HALF, HALF), HALF)

    def pair(j, _):
        relay_copy(j).wait_recv()
        whole = table[j]
        high = whole.astype(BF)
        split[0:512] = high
        split[512:1024] = (whole - high.astype(F32)).astype(BF)
        pulled = (pulled0, pulled1)
        gather(0, pulled[0])
        for b in range(blocks - 1):
            gather(b + 1, pulled[(b + 1) % 2])
            combine(j, b, pulled[b % 2])
            if b == 0:
                pl.when(j > 0)(lambda: to_owners(j - 1))
                pl.when(j == 0)(lambda: spread(3))

        pl.when(j + 1 < PAIRS)(lambda: relay(j + 1))
        pl.semaphore_wait(ready.at[j], 2)
        pl.when(j + 1 < PAIRS)(lambda: heard(j + 1))
        sums[j, theirs, :] = scatter(theirs, early)
        sums[j, mine, :] = scatter(mine, early)
        combine(j, blocks - 1, pulled[(blocks - 1) % 2])
        sums[j, theirs, :] += scatter(theirs, late)
        core_copy(j).start()
        sums[j, mine, :] += scatter(mine, late)
        return 0

    lax.fori_loop(0, PAIRS, pair, 0)
    to_owners(PAIRS - 1)

    load_dual.wait()
    load_coeffs.wait()
    co = [coeffs_ref[t] for t in range(TERMS)]
    co_re = [jnp.where(low, v, swap_halves(v)) for v in co]
    co_im = [jnp.where(low, swap_halves(v), v) for v in co]
    half_lane = lax.broadcasted_iota(jnp.int32, (1, 128), 1)
    total = [jnp.zeros((OWN, 128), F32) for _ in range(TERMS)]
    for j in range(PAIRS):
        all_in(j).wait_recv()
        normal = chip_sum[j, pl.ds(pl.multiple_of(m * OWN, OWN), OWN)]
        for d in range(CHIPS - 1):
            normal = normal + chip_in[j, d]
        f0 = k * 8 + 2 * j
        p0 = jnp.full((1, 128), pen_smem[f0], jnp.int32)
        p1 = jnp.full((1, 128), pen_smem[f0 + 1], jnp.int32)
        w0 = 4.0 * p0.astype(F32)
        w1 = 4.0 * p1.astype(F32)
        spot0 = (jnp.full((1, 128), f0, jnp.int32).astype(F32) + 0.5) / 128.0
        spot1 = (jnp.full((1, 128), f0 + 1, jnp.int32).astype(F32) + 0.5) / 128.0
        b0, b1 = bernstein(spot0), bernstein(spot1)
        weight = jnp.where(half_lane < 64, w0, w1)
        both = [jnp.where(half_lane < 64, u, v) for u, v in zip(b0, b1)]
        d0, d1 = dual_ref[2 * j], dual_ref[2 * j + 1]
        dual_re = jnp.where(low, d0, swap_halves(d1))
        dual_im = jnp.where(low, swap_halves(d0), d1)
        prior_re = sum(both[t] * co_re[t] for t in range(TERMS))
        prior_im = sum(both[t] * co_im[t] for t in range(TERMS))
        under = normal[:, 256:384] + weight
        gain_re = (normal[:, 0:128] + weight * (prior_re - dual_re)) / under
        gain_im = (normal[:, 128:256] + weight * (prior_im - dual_im)) / under
        g0 = jnp.where(low, gain_re, swap_halves(gain_im))
        g1 = jnp.where(low, swap_halves(gain_re), gain_im)
        ng_ref[2 * j] = g0
        ng_ref[2 * j + 1] = g1
        for t in range(TERMS):
            total[t] = total[t] + (w0 * b0[t]) * (g0 + d0) + (w1 * b1[t]) * (g1 + d1)

    out_gains = pltpu.make_async_copy(ng_ref, ng_hbm, out_sem.at[0])
    out_gains.start()
    out_fac = pltpu.make_async_copy(fac, fac_hbm, out_sem.at[1])
    out_fac.start()
    for t in range(TERMS):
        mom[4 * t:4 * t + 4] = total[t].reshape(4, 8, 128)
    for slot, hop in enumerate(SUB_HOPS):
        pltpu.make_async_remote_copy(
            src_ref=mom.at[sub_at(hop)], dst_ref=mom_in.at[slot],
            send_sem=m_send, recv_sem=m_recv, device_id=sub_peer(hop), device_id_type=MESH,
        ).start()
    m_all = pltpu.make_async_remote_copy(
        src_ref=mom_in, dst_ref=mom_in, send_sem=m_send, recv_sem=m_recv,
        device_id=other, device_id_type=MESH,
    )
    m_all.wait_recv()
    tile = mom[k]
    for d in range(SUBS - 1):
        tile = tile + mom_in[d]
    mom_all[k] = tile
    for hop in SUB_HOPS:
        pltpu.make_async_remote_copy(
            src_ref=mom_all.at[k], dst_ref=mom_all.at[k],
            send_sem=r_send, recv_sem=r_recv, device_id=sub_peer(hop), device_id_type=MESH,
        ).start()
    r_all = pltpu.make_async_remote_copy(
        src_ref=mom_all.at[pl.ds(0, SUBS - 1)], dst_ref=mom_all.at[pl.ds(0, SUBS - 1)],
        send_sem=r_send, recv_sem=r_recv, device_id=other, device_id_type=MESH,
    )
    r_all.wait_recv()

    out_mom = pltpu.make_async_copy(mom_all, mom_hbm, out_sem.at[2])
    out_mom.start()

    for j in range(PAIRS):
        sent = table.at[j, pl.ds(0, (CHIPS - 1) * OWN)]
        pltpu.make_async_remote_copy(
            src_ref=sent, dst_ref=sent, send_sem=ag_send.at[j], recv_sem=ag_recv.at[j],
            device_id=other, device_id_type=MESH,
        ).wait_send()
        relay_copy(j).wait_send()
        core_copy(j).wait_send()
        all_in(j).wait_send()
    m_all.wait_send()
    r_all.wait_send()
    out_gains.wait()
    out_fac.wait()
    out_mom.wait()


def finish(ng_ref, dual_ref, mom_all, fac, ng_out, nd_ref, nc_ref):
    k = lax.axis_index("sub")
    low_of = lambda r, q: fac[4 * r + q:4 * r + q + 1, :]
    forward = []
    for r in range(TERMS):
        value = mom_all[4 * r:4 * r + 4].reshape(OWN, 128)
        for q in range(r):
            value = value - low_of(r, q) * forward[q]
        forward.append(value / low_of(r, r))
    back = [None] * TERMS
    for r in range(TERMS - 1, -1, -1):
        value = forward[r]
        for q in range(r + 1, TERMS):
            value = value - low_of(q, r) * back[q]
        back[r] = value / low_of(r, r)
        nc_ref[r] = back[r]
    for f in range(2 * PAIRS):
        spot = (jnp.full((1, 128), k * 8 + f, jnp.int32).astype(F32) + 0.5) / 128.0
        basis = bernstein(spot)
        agreed = sum(basis[t] * back[t] for t in range(TERMS))
        gain = ng_ref[f]
        ng_out[f] = gain
        nd_ref[f] = dual_ref[f] + gain - agreed


def step(coherency, visibility, stations, gains, dual, coeffs, penalty):
    vmem = pl.BlockSpec(memory_space=pltpu.VMEM)
    hbm = pl.BlockSpec(memory_space=pl.ANY)
    dma = pltpu.SemaphoreType.DMA
    gained, moments, factor = pl.pallas_call(
        kernel,
        out_shape=(
            jax.ShapeDtypeStruct(gains.shape, F32),
            jax.ShapeDtypeStruct((SUBS, 8, 128), F32),
            jax.ShapeDtypeStruct((16, 128), F32),
        ),
        in_specs=[hbm, hbm, hbm, hbm, hbm, hbm, vmem, pl.BlockSpec(memory_space=pltpu.SMEM)],
        out_specs=(hbm, hbm, hbm),
        scratch_shapes=[
            pltpu.VMEM((8, BASE, 128), BF),
            pltpu.VMEM((2, 8, BASE), F32),
            pltpu.VMEM((8, OWN, 128), F32),
            pltpu.VMEM((8, OWN, 128), F32),
            pltpu.VMEM((TERMS, OWN, 128), F32),
            pltpu.VMEM((2, BASE), jnp.int32),
            pltpu.VMEM((8, OWN, 128), F32),
            pltpu.VMEM((128, BASE), F32),
            pltpu.VMEM((BASE, 128), BF),
            pltpu.VMEM((2 * BASE, STATIONS), BF),
            pltpu.VMEM((STATIONS, BASE), BF),
            pltpu.VMEM((STATIONS, BASE), BF),
            pltpu.VMEM((PAIRS, 640, 256), BF),
            pltpu.VMEM((PAIRS, STATIONS, 256), F32),
            pltpu.VMEM((2 * STATIONS, 256), BF),
            pltpu.VMEM((2 * BLOCK, 256), F32),
            pltpu.VMEM((2 * BLOCK, 256), F32),
            pltpu.VMEM((BASE, 384), BF),
            pltpu.VMEM((BASE, 384), BF),
            pltpu.VMEM((PAIRS, STATIONS, 384), F32),
            pltpu.VMEM((PAIRS, HALF, 384), F32),
            pltpu.VMEM((PAIRS, HALF, 384), F32),
            pltpu.VMEM((PAIRS, CHIPS - 1, OWN, 384), F32),
            pltpu.VMEM((SUBS, 8, 128), F32),
            pltpu.VMEM((SUBS - 1, 8, 128), F32),
            pltpu.VMEM((SUBS, 8, 128), F32),
            pltpu.VMEM((16, 128), F32),
            pltpu.SemaphoreType.REGULAR((PAIRS,)), dma((6,)), dma((3,)),
            dma((PAIRS,)), dma((PAIRS,)),
            dma((PAIRS,)), dma((PAIRS,)),
            dma((PAIRS,)), dma((PAIRS,)),
            dma((PAIRS,)), dma((PAIRS,)),
            dma(()), dma(()), dma(()), dma(()),
        ],
        compiler_params=pltpu.CompilerParams(
            collective_id=0, has_side_effects=True, vmem_limit_bytes=56 * 1024 * 1024
        ),
    )(coherency, visibility, gains, dual, coeffs, stations, penalty.reshape(1, 128), penalty)
    return pl.pallas_call(
        finish,
        out_shape=(
            jax.ShapeDtypeStruct(gains.shape, F32),
            jax.ShapeDtypeStruct(gains.shape, F32),
            jax.ShapeDtypeStruct(coeffs.shape, F32),
        ),
        in_specs=[vmem] * 4,
        out_specs=(vmem,) * 3,
    )(gained, dual, moments, factor)


def solution(mesh):
    placed = (
        P("sub", "bl", None),
        P(None, "sub", "bl"),
        P(None, "bl"),
        P("sub", "bl", None),
        P("sub", "bl", None),
        P(None, "bl", None),
        P(),
    )
    return jax.shard_map(
        step,
        mesh=mesh,
        in_specs=placed,
        out_specs=(P("sub", "bl", None), P("sub", "bl", None), P(None, "bl", None)),
        check_vma=False,
    )
```

```python
import functools
import math

import jax
import jax.numpy as jnp
from jax import lax
from jax.experimental import pallas as pl
from jax.experimental.pallas import tpu as pltpu
from jax.sharding import PartitionSpec as P

MESH = pl.DeviceIdType.MESH
BF = jnp.bfloat16
F32 = jnp.float32
F8 = jnp.float8_e5m2
FINE = 256.0
PAIRS = 4
STATIONS = 512
HALF = 256
OWN = 32
BASE = 2048
CHIPS = 8
SUBS = 16
TERMS = 4
BLOCK = 512
CHIP_HOPS = ((2, 1), (2, 0), (1, 1), (3, 1), (0, 1), (1, 0), (3, 0))
SUB_HOPS = (
    (1, 4), (0, 4), (1, 3), (1, 5), (0, 3), (0, 5), (1, 2), (1, 6),
    (0, 2), (0, 6), (1, 1), (1, 7), (0, 1), (0, 7), (1, 0),
)


def bernstein(position):
    degree = TERMS - 1
    rest = 1.0 - position
    out = []
    for order in range(TERMS):
        value = jnp.full_like(position, float(math.comb(degree, order)))
        for _ in range(order):
            value = value * position
        for _ in range(degree - order):
            value = value * rest
        out.append(value)
    return out


def swap_halves(value):
    return pltpu.roll(value, 64, 1)


def kernel(
    coh_hbm, vis_hbm, gains_hbm, dual_hbm, coeffs_hbm, stations_hbm, pen_row, pen_smem,
    ng_hbm, mom_hbm, fac_hbm,
    coh, vis, gains_ref, dual_ref, coeffs_ref, stations_ref, ng_ref,
    wide, colb, hot, hot_pt, hot_qt, mix,
    table, split, fine, hot_fine, pulled0, pulled1, terms_p, terms_q, sums, core_in, chip_sum, chip_in,
    mom, mom_in, mom_all, fac,
    ready, load_sem, out_sem, ag_send, ag_recv, relay_send, relay_recv, core_send, core_recv,
    rs_send, rs_recv, m_send, m_recv, r_send, r_recv,
):
    k = lax.axis_index("sub")
    i = lax.axis_index("bl")
    m = i // 2
    c = i % 2
    other = (k, m * 2 + (1 - c))

    def chip_at(hop):
        return lax.rem(m // 2 + hop[0], 4) * 2 + lax.rem(m + hop[1], 2)

    def chip_peer(hop):
        return (k, chip_at(hop) * 2 + c)

    def sub_at(hop):
        return lax.rem(k // 8 + hop[0], 2) * 8 + lax.rem(k + hop[1], 8)

    def sub_peer(hop):
        return (sub_at(hop), i)

    barrier = pltpu.get_barrier_semaphore()
    pl.semaphore_signal(barrier, inc=1, device_id=other, device_id_type=MESH)
    for hop in CHIP_HOPS:
        pl.semaphore_signal(barrier, inc=1, device_id=chip_peer(hop), device_id_type=MESH)
    above, below = sub_peer((0, 1)), sub_peer((0, 7))
    for near in (above, below, sub_peer((1, 0))):
        pl.semaphore_signal(barrier, inc=1, device_id=near, device_id_type=MESH)

    load_gains = pltpu.make_async_copy(gains_hbm, gains_ref, load_sem.at[2])
    load_gains.start()
    load_stations = pltpu.make_async_copy(stations_hbm, stations_ref, load_sem.at[3])
    load_stations.start()
    load_vis = pltpu.make_async_copy(vis_hbm, vis, load_sem.at[0])
    load_vis.start()
    load_coh = pltpu.make_async_copy(coh_hbm, coh, load_sem.at[1])
    load_coh.start()
    load_dual = pltpu.make_async_copy(dual_hbm, dual_ref, load_sem.at[4])
    load_dual.start()
    load_coeffs = pltpu.make_async_copy(coeffs_hbm, coeffs_ref, load_sem.at[5])
    load_coeffs.start()

    low = lax.broadcasted_iota(jnp.int32, (OWN, 128), 1) < 64
    load_gains.wait()
    own_row = pl.multiple_of(c * HALF + m * OWN, OWN)
    for j in range(PAIRS):
        first, second = gains_ref[2 * j], gains_ref[2 * j + 1]
        table[j, pl.ds(own_row, OWN), 0:128] = jnp.where(low, first, swap_halves(second))
        table[j, pl.ds(own_row, OWN), 128:256] = jnp.where(low, swap_halves(first), second)

    pl.semaphore_wait(barrier, 1 + (CHIPS - 1) + 3)

    def spread(j):
        for hop in CHIP_HOPS:
            rows = table.at[j, pl.ds(own_row, OWN)]
            pltpu.make_async_remote_copy(
                src_ref=rows, dst_ref=rows, send_sem=ag_send.at[j], recv_sem=ag_recv.at[j],
                device_id=chip_peer(hop), device_id_type=MESH,
            ).start()

    def heard(j):
        for near in (above, below):
            pl.semaphore_signal(ready.at[j], inc=1, device_id=near, device_id_type=MESH)

    spread(0)
    heard(0)

    load_stations.wait()
    raw = stations_ref[...]
    spot = ((raw >> 5) & 1) * HALF + (raw >> 6) * OWN + (raw & 31)
    load_vis.wait()
    spot_f = spot.astype(F32)
    seen = vis[...].reshape(16, BASE)
    coarse = seen.astype(BF).astype(F32)
    wide[...] = jnp.zeros_like(wide)
    wide[0:16] = coarse
    wide[16:32] = seen - coarse
    wide[32:34] = spot_f

    def turn(t, _):
        at = pl.ds(pl.multiple_of(t * 128, 128), 128)
        piece = wide[:, at].T
        colb[at, :] = piece.astype(BF)
        lane = lax.broadcasted_iota(jnp.int32, (128, STATIONS), 1).astype(F32)
        per = BLOCK // 128
        for end in range(2):
            to = pl.ds(pl.multiple_of(((t // per) * 2 + end) * BLOCK + (t % per) * 128, 128), 128)
            match = piece[:, 32 + end:33 + end] == lane
            hot[to, :] = jnp.where(match, 1.0, 0.0).astype(BF)
            hot_fine[to, :] = jnp.where(match, 1.0 / FINE, 0.0).astype(F8)
        return 0

    lax.fori_loop(0, BASE // 128, turn, 0)

    def turn_t(t, _):
        at = pl.ds(pl.multiple_of(t * 32, 32), 32)
        row = (lax.broadcasted_iota(jnp.int32, (32, BASE), 0) + t * 32).astype(F32)
        hot_pt[at, :] = jnp.where(wide[32:33, :] == row, 1.0, 0.0).astype(BF)
        hot_qt[at, :] = jnp.where(wide[33:34, :] == row, 1.0, 0.0).astype(BF)
        return 0

    lax.fori_loop(0, STATIONS // 32, turn_t, 0)

    spread(1)
    out_lane = lax.broadcasted_iota(jnp.int32, (128, 256), 1)
    in_row = lax.broadcasted_iota(jnp.int32, (128, 256), 0)
    in_lane = lax.broadcasted_iota(jnp.int32, (256, 256), 0)
    out_wide = lax.broadcasted_iota(jnp.int32, (256, 256), 1)
    for j in range(PAIRS):
        want = (out_lane // 128) * 8 + 2 * j + (out_lane // 64) % 2
        hit = (in_row < 32) & (in_row % 16 == want)
        minus = jnp.where(in_lane // 64 == out_wide // 64, -1.0, 0.0).astype(BF)
        mix[j, 0:256] = minus
        mix[j, 256:512] = minus
        mix[j, 512:640] = jnp.where(hit, 1.0, 0.0).astype(BF)

    channel = lax.broadcasted_iota(jnp.int32, (1, 128), 1).astype(F32)
    rows_b = bernstein((channel + 0.5) / 128.0)
    weight_row = 4.0 * pen_row[...].astype(F32)
    lower = {}
    for r in range(TERMS):
        for q in range(r + 1):
            value = jnp.sum(weight_row * rows_b[r] * rows_b[q], axis=1, keepdims=True)
            for s in range(q):
                value = value - lower[r, s] * lower[q, s]
            lower[r, q] = jnp.sqrt(value) if r == q else value / lower[q, q]
            fac[4 * r + q:4 * r + q + 1, :] = jnp.broadcast_to(lower[r, q], (1, 128))

    load_coh.wait()

    def relay(j):
        got = table.at[j, pl.ds(0, (CHIPS - 1) * OWN)]
        pltpu.make_async_remote_copy(
            src_ref=got, dst_ref=got, send_sem=ag_send.at[j], recv_sem=ag_recv.at[j],
            device_id=other, device_id_type=MESH,
        ).wait_recv()
        half = table.at[j, pl.ds(pl.multiple_of(c * HALF, HALF), HALF)]
        pltpu.make_async_remote_copy(
            src_ref=half, dst_ref=half, send_sem=relay_send.at[j], recv_sem=relay_recv.at[j],
            device_id=other, device_id_type=MESH,
        ).start()

    def relay_copy(j):
        half = table.at[j, pl.ds(pl.multiple_of(c * HALF, HALF), HALF)]
        return pltpu.make_async_remote_copy(
            src_ref=half, dst_ref=half, send_sem=relay_send.at[j], recv_sem=relay_recv.at[j],
            device_id=other, device_id_type=MESH,
        )

    def core_copy(j):
        return pltpu.make_async_remote_copy(
            src_ref=sums.at[j, pl.ds(pl.multiple_of((1 - c) * HALF, HALF), HALF)],
            dst_ref=core_in.at[j], send_sem=core_send.at[j], recv_sem=core_recv.at[j],
            device_id=other, device_id_type=MESH,
        )

    def to_owners(j):
        core_copy(j).wait_recv()
        chip_sum[j] = sums[j, pl.ds(pl.multiple_of(c * HALF, HALF), HALF)] + core_in[j]
        for slot, hop in enumerate(CHIP_HOPS):
            owner = chip_at(hop)
            pltpu.make_async_remote_copy(
                src_ref=chip_sum.at[j, pl.ds(pl.multiple_of(owner * OWN, OWN), OWN)],
                dst_ref=chip_in.at[j, slot], send_sem=rs_send.at[j], recv_sem=rs_recv.at[j],
                device_id=chip_peer(hop), device_id_type=MESH,
            ).start()

    def all_in(j):
        return pltpu.make_async_remote_copy(
            src_ref=chip_in.at[j], dst_ref=chip_in.at[j], send_sem=rs_send.at[j],
            recv_sem=rs_recv.at[j], device_id=other, device_id_type=MESH,
        )

    wide_low = lax.broadcasted_iota(jnp.int32, (BLOCK, 128), 1) < 64

    relay(0)
    spread(2)

    def gather(b, pulled):
        at = slice(b * 2 * BLOCK, (b + 1) * 2 * BLOCK)
        pulled[...] = jnp.dot(hot[at, :], split[...], preferred_element_type=F32) + jnp.dot(
            hot_fine[at, :], fine[...], preferred_element_type=F32
        )

    def combine(j, b, pulled):
        at = slice(b * BLOCK, (b + 1) * BLOCK)
        c0 = coh[2 * j, at, :].astype(F32)
        c1 = coh[2 * j + 1, at, :].astype(F32)
        cr = jnp.where(wide_low, c0, swap_halves(c1))
        ci = jnp.where(wide_low, swap_halves(c0), c1)
        nr, ni = pulled[0:BLOCK, 0:128], pulled[0:BLOCK, 128:256]
        fr, fi = pulled[BLOCK:2 * BLOCK, 0:128], pulled[BLOCK:2 * BLOCK, 128:256]
        hr = cr * fr + ci * fi
        hi = ci * fr - cr * fi
        mr = nr * hr - ni * hi
        mi = nr * hi + ni * hr
        mrh, mih = mr.astype(BF), mi.astype(BF)
        mrl = (mr - mrh.astype(F32)).astype(BF)
        mil = (mi - mih.astype(F32)).astype(BF)
        resid = jnp.dot(
            jnp.concatenate([mrh, mih, mrl, mil, colb[at, :]], 1), mix[j],
            preferred_element_type=F32,
        )
        tr = resid[:, 0:128] + mr
        ti = resid[:, 128:256] + mi
        er = cr * nr - ci * ni
        ei = cr * ni + ci * nr
        terms_p[at, 0:128] = (tr * hr + ti * hi).astype(BF)
        terms_p[at, 128:256] = (ti * hr - tr * hi).astype(BF)
        terms_p[at, 256:384] = (hr * hr + hi * hi).astype(BF)
        terms_q[at, 0:128] = (tr * er + ti * ei).astype(BF)
        terms_q[at, 128:256] = (tr * ei - ti * er).astype(BF)
        terms_q[at, 256:384] = (er * er + ei * ei).astype(BF)

    def scatter(rows, at):
        return jnp.dot(
            hot_pt[rows, at], terms_p[at, :], preferred_element_type=F32
        ) + jnp.dot(hot_qt[rows, at], terms_q[at, :], preferred_element_type=F32)

    blocks = BASE // BLOCK
    early = slice(0, BASE - BLOCK)
    late = slice(BASE - BLOCK, BASE)
    theirs = pl.ds(pl.multiple_of((1 - c) * HALF, HALF), HALF)
    mine = pl.ds(pl.multiple_of(c * HALF, HALF), HALF)

    def pair(j, _):
        relay_copy(j).wait_recv()
        whole = table[j]
        high = whole.astype(BF)
        split[...] = high
        fine[...] = ((whole - high.astype(F32)) * FINE).astype(F8)
        pulled = (pulled0, pulled1)
        gather(0, pulled[0])
        for b in range(blocks - 1):
            gather(b + 1, pulled[(b + 1) % 2])
            combine(j, b, pulled[b % 2])
            if b == 0:
                pl.when(j > 0)(lambda: to_owners(j - 1))
                pl.when(j == 0)(lambda: spread(3))

        pl.when(j + 1 < PAIRS)(lambda: relay(j + 1))
        pl.semaphore_wait(ready.at[j], 2)
        pl.when(j + 1 < PAIRS)(lambda: heard(j + 1))
        sums[j] = scatter(slice(0, STATIONS), early)
        combine(j, blocks - 1, pulled[(blocks - 1) % 2])
        sums[j, theirs, :] += scatter(theirs, late)
        core_copy(j).start()
        sums[j, mine, :] += scatter(mine, late)
        return 0

    lax.fori_loop(0, PAIRS, pair, 0)
    to_owners(PAIRS - 1)

    load_dual.wait()
    load_coeffs.wait()
    co = [coeffs_ref[t] for t in range(TERMS)]
    co_re = [jnp.where(low, v, swap_halves(v)) for v in co]
    co_im = [jnp.where(low, swap_halves(v), v) for v in co]
    half_lane = lax.broadcasted_iota(jnp.int32, (1, 128), 1)
    total = [jnp.zeros((OWN, 128), F32) for _ in range(TERMS)]
    for j in range(PAIRS):
        all_in(j).wait_recv()
        normal = chip_sum[j, pl.ds(pl.multiple_of(m * OWN, OWN), OWN)]
        for d in range(CHIPS - 1):
            normal = normal + chip_in[j, d]
        f0 = k * 8 + 2 * j
        p0 = jnp.full((1, 128), pen_smem[f0], jnp.int32)
        p1 = jnp.full((1, 128), pen_smem[f0 + 1], jnp.int32)
        w0 = 4.0 * p0.astype(F32)
        w1 = 4.0 * p1.astype(F32)
        spot0 = (jnp.full((1, 128), f0, jnp.int32).astype(F32) + 0.5) / 128.0
        spot1 = (jnp.full((1, 128), f0 + 1, jnp.int32).astype(F32) + 0.5) / 128.0
        b0, b1 = bernstein(spot0), bernstein(spot1)
        weight = jnp.where(half_lane < 64, w0, w1)
        both = [jnp.where(half_lane < 64, u, v) for u, v in zip(b0, b1)]
        d0, d1 = dual_ref[2 * j], dual_ref[2 * j + 1]
        dual_re = jnp.where(low, d0, swap_halves(d1))
        dual_im = jnp.where(low, swap_halves(d0), d1)
        prior_re = sum(both[t] * co_re[t] for t in range(TERMS))
        prior_im = sum(both[t] * co_im[t] for t in range(TERMS))
        under = normal[:, 256:384] + weight
        gain_re = (normal[:, 0:128] + weight * (prior_re - dual_re)) / under
        gain_im = (normal[:, 128:256] + weight * (prior_im - dual_im)) / under
        g0 = jnp.where(low, gain_re, swap_halves(gain_im))
        g1 = jnp.where(low, swap_halves(gain_re), gain_im)
        ng_ref[2 * j] = g0
        ng_ref[2 * j + 1] = g1
        for t in range(TERMS):
            total[t] = total[t] + (w0 * b0[t]) * (g0 + d0) + (w1 * b1[t]) * (g1 + d1)

    out_gains = pltpu.make_async_copy(ng_ref, ng_hbm, out_sem.at[0])
    out_gains.start()
    out_fac = pltpu.make_async_copy(fac, fac_hbm, out_sem.at[1])
    out_fac.start()
    for t in range(TERMS):
        mom[4 * t:4 * t + 4] = total[t].reshape(4, 8, 128)
    for slot, hop in enumerate(SUB_HOPS):
        pltpu.make_async_remote_copy(
            src_ref=mom.at[sub_at(hop)], dst_ref=mom_in.at[slot],
            send_sem=m_send, recv_sem=m_recv, device_id=sub_peer(hop), device_id_type=MESH,
        ).start()
    m_all = pltpu.make_async_remote_copy(
        src_ref=mom_in, dst_ref=mom_in, send_sem=m_send, recv_sem=m_recv,
        device_id=other, device_id_type=MESH,
    )
    m_all.wait_recv()
    tile = mom[k]
    for d in range(SUBS - 1):
        tile = tile + mom_in[d]
    mom_all[k] = tile
    for hop in SUB_HOPS:
        pltpu.make_async_remote_copy(
            src_ref=mom_all.at[k], dst_ref=mom_all.at[k],
            send_sem=r_send, recv_sem=r_recv, device_id=sub_peer(hop), device_id_type=MESH,
        ).start()
    r_all = pltpu.make_async_remote_copy(
        src_ref=mom_all.at[pl.ds(0, SUBS - 1)], dst_ref=mom_all.at[pl.ds(0, SUBS - 1)],
        send_sem=r_send, recv_sem=r_recv, device_id=other, device_id_type=MESH,
    )
    r_all.wait_recv()

    out_mom = pltpu.make_async_copy(mom_all, mom_hbm, out_sem.at[2])
    out_mom.start()

    for j in range(PAIRS):
        sent = table.at[j, pl.ds(0, (CHIPS - 1) * OWN)]
        pltpu.make_async_remote_copy(
            src_ref=sent, dst_ref=sent, send_sem=ag_send.at[j], recv_sem=ag_recv.at[j],
            device_id=other, device_id_type=MESH,
        ).wait_send()
        relay_copy(j).wait_send()
        core_copy(j).wait_send()
        all_in(j).wait_send()
    m_all.wait_send()
    r_all.wait_send()
    out_gains.wait()
    out_fac.wait()
    out_mom.wait()


def finish(ng_ref, dual_ref, mom_all, fac, ng_out, nd_ref, nc_ref):
    k = lax.axis_index("sub")
    low_of = lambda r, q: fac[4 * r + q:4 * r + q + 1, :]
    forward = []
    for r in range(TERMS):
        value = mom_all[4 * r:4 * r + 4].reshape(OWN, 128)
        for q in range(r):
            value = value - low_of(r, q) * forward[q]
        forward.append(value / low_of(r, r))
    back = [None] * TERMS
    for r in range(TERMS - 1, -1, -1):
        value = forward[r]
        for q in range(r + 1, TERMS):
            value = value - low_of(q, r) * back[q]
        back[r] = value / low_of(r, r)
        nc_ref[r] = back[r]
    for f in range(2 * PAIRS):
        spot = (jnp.full((1, 128), k * 8 + f, jnp.int32).astype(F32) + 0.5) / 128.0
        basis = bernstein(spot)
        agreed = sum(basis[t] * back[t] for t in range(TERMS))
        gain = ng_ref[f]
        ng_out[f] = gain
        nd_ref[f] = dual_ref[f] + gain - agreed


def step(coherency, visibility, stations, gains, dual, coeffs, penalty):
    vmem = pl.BlockSpec(memory_space=pltpu.VMEM)
    hbm = pl.BlockSpec(memory_space=pl.ANY)
    dma = pltpu.SemaphoreType.DMA
    gained, moments, factor = pl.pallas_call(
        kernel,
        out_shape=(
            jax.ShapeDtypeStruct(gains.shape, F32),
            jax.ShapeDtypeStruct((SUBS, 8, 128), F32),
            jax.ShapeDtypeStruct((16, 128), F32),
        ),
        in_specs=[hbm, hbm, hbm, hbm, hbm, hbm, vmem, pl.BlockSpec(memory_space=pltpu.SMEM)],
        out_specs=(hbm, hbm, hbm),
        scratch_shapes=[
            pltpu.VMEM((8, BASE, 128), BF),
            pltpu.VMEM((2, 8, BASE), F32),
            pltpu.VMEM((8, OWN, 128), F32),
            pltpu.VMEM((8, OWN, 128), F32),
            pltpu.VMEM((TERMS, OWN, 128), F32),
            pltpu.VMEM((2, BASE), jnp.int32),
            pltpu.VMEM((8, OWN, 128), F32),
            pltpu.VMEM((128, BASE), F32),
            pltpu.VMEM((BASE, 128), BF),
            pltpu.VMEM((2 * BASE, STATIONS), BF),
            pltpu.VMEM((STATIONS, BASE), BF),
            pltpu.VMEM((STATIONS, BASE), BF),
            pltpu.VMEM((PAIRS, 640, 256), BF),
            pltpu.VMEM((PAIRS, STATIONS, 256), F32),
            pltpu.VMEM((STATIONS, 256), BF),
            pltpu.VMEM((STATIONS, 256), F8),
            pltpu.VMEM((2 * BASE, STATIONS), F8),
            pltpu.VMEM((2 * BLOCK, 256), F32),
            pltpu.VMEM((2 * BLOCK, 256), F32),
            pltpu.VMEM((BASE, 384), BF),
            pltpu.VMEM((BASE, 384), BF),
            pltpu.VMEM((PAIRS, STATIONS, 384), F32),
            pltpu.VMEM((PAIRS, HALF, 384), F32),
            pltpu.VMEM((PAIRS, HALF, 384), F32),
            pltpu.VMEM((PAIRS, CHIPS - 1, OWN, 384), F32),
            pltpu.VMEM((SUBS, 8, 128), F32),
            pltpu.VMEM((SUBS - 1, 8, 128), F32),
            pltpu.VMEM((SUBS, 8, 128), F32),
            pltpu.VMEM((16, 128), F32),
            pltpu.SemaphoreType.REGULAR((PAIRS,)), dma((6,)), dma((3,)),
            dma((PAIRS,)), dma((PAIRS,)),
            dma((PAIRS,)), dma((PAIRS,)),
            dma((PAIRS,)), dma((PAIRS,)),
            dma((PAIRS,)), dma((PAIRS,)),
            dma(()), dma(()), dma(()), dma(()),
        ],
        compiler_params=pltpu.CompilerParams(
            collective_id=0, has_side_effects=True, vmem_limit_bytes=56 * 1024 * 1024
        ),
    )(coherency, visibility, gains, dual, coeffs, stations, penalty.reshape(1, 128), penalty)
    return pl.pallas_call(
        finish,
        out_shape=(
            jax.ShapeDtypeStruct(gains.shape, F32),
            jax.ShapeDtypeStruct(gains.shape, F32),
            jax.ShapeDtypeStruct(coeffs.shape, F32),
        ),
        in_specs=[vmem] * 4,
        out_specs=(vmem,) * 3,
    )(gained, dual, moments, factor)


def solution(mesh):
    placed = (
        P("sub", "bl", None),
        P(None, "sub", "bl"),
        P(None, "bl"),
        P("sub", "bl", None),
        P("sub", "bl", None),
        P(None, "bl", None),
        P(),
    )
    return jax.shard_map(
        step,
        mesh=mesh,
        in_specs=placed,
        out_specs=(P("sub", "bl", None), P("sub", "bl", None), P(None, "bl", None)),
        check_vma=False,
    )
```

```python
import functools
import math

import jax
import jax.numpy as jnp
from jax import lax
from jax.experimental import pallas as pl
from jax.experimental.pallas import tpu as pltpu
from jax.sharding import PartitionSpec as P

MESH = pl.DeviceIdType.MESH
BF = jnp.bfloat16
F32 = jnp.float32
F8 = jnp.float8_e5m2
FINE = 256.0
PAIRS = 4
STATIONS = 512
HALF = 256
OWN = 32
BASE = 2048
CHIPS = 8
SUBS = 16
TERMS = 4
BLOCK = 512
CHIP_HOPS = ((2, 1), (2, 0), (1, 1), (3, 1), (0, 1), (1, 0), (3, 0))
SUB_HOPS = (
    (1, 4), (0, 4), (1, 3), (1, 5), (0, 3), (0, 5), (1, 2), (1, 6),
    (0, 2), (0, 6), (1, 1), (1, 7), (0, 1), (0, 7), (1, 0),
)


def bernstein(position):
    degree = TERMS - 1
    rest = 1.0 - position
    out = []
    for order in range(TERMS):
        value = jnp.full_like(position, float(math.comb(degree, order)))
        for _ in range(order):
            value = value * position
        for _ in range(degree - order):
            value = value * rest
        out.append(value)
    return out


def swap_halves(value):
    return pltpu.roll(value, 64, 1)


def kernel(
    coh_hbm, vis_hbm, gains_hbm, dual_hbm, coeffs_hbm, stations_hbm, pen_row, pen_smem,
    ng_hbm, mom_hbm, fac_hbm,
    coh, packed, vis, gains_ref, dual_ref, coeffs_ref, stations_ref, ng_ref,
    wide, colb, hot, hot_pt, hot_qt, mix,
    table, split, fine, hot_fine, pulled0, pulled1, terms_p, terms_q, sums, core_in, chip_sum, chip_in,
    mom, mom_in, mom_all, fac,
    ready, load_sem, out_sem, ag_send, ag_recv, relay_send, relay_recv, core_send, core_recv,
    rs_send, rs_recv, m_send, m_recv, r_send, r_recv,
):
    k = lax.axis_index("sub")
    i = lax.axis_index("bl")
    m = i // 2
    c = i % 2
    other = (k, m * 2 + (1 - c))

    def chip_at(hop):
        return lax.rem(m // 2 + hop[0], 4) * 2 + lax.rem(m + hop[1], 2)

    def chip_peer(hop):
        return (k, chip_at(hop) * 2 + c)

    def sub_at(hop):
        return lax.rem(k // 8 + hop[0], 2) * 8 + lax.rem(k + hop[1], 8)

    def sub_peer(hop):
        return (sub_at(hop), i)

    barrier = pltpu.get_barrier_semaphore()
    pl.semaphore_signal(barrier, inc=1, device_id=other, device_id_type=MESH)
    for hop in CHIP_HOPS:
        pl.semaphore_signal(barrier, inc=1, device_id=chip_peer(hop), device_id_type=MESH)
    above, below = sub_peer((0, 1)), sub_peer((0, 7))
    for near in (above, below, sub_peer((1, 0))):
        pl.semaphore_signal(barrier, inc=1, device_id=near, device_id_type=MESH)

    load_gains = pltpu.make_async_copy(gains_hbm, gains_ref, load_sem.at[2])
    load_gains.start()
    load_stations = pltpu.make_async_copy(stations_hbm, stations_ref, load_sem.at[3])
    load_stations.start()
    load_vis = pltpu.make_async_copy(vis_hbm, vis, load_sem.at[0])
    load_vis.start()
    load_coh = pltpu.make_async_copy(coh_hbm, coh, load_sem.at[1])
    load_coh.start()
    load_dual = pltpu.make_async_copy(dual_hbm, dual_ref, load_sem.at[4])
    load_dual.start()
    load_coeffs = pltpu.make_async_copy(coeffs_hbm, coeffs_ref, load_sem.at[5])
    load_coeffs.start()

    low = lax.broadcasted_iota(jnp.int32, (OWN, 128), 1) < 64
    load_gains.wait()
    own_row = pl.multiple_of(c * HALF + m * OWN, OWN)
    for j in range(PAIRS):
        first, second = gains_ref[2 * j], gains_ref[2 * j + 1]
        table[j, pl.ds(own_row, OWN), 0:128] = jnp.where(low, first, swap_halves(second))
        table[j, pl.ds(own_row, OWN), 128:256] = jnp.where(low, swap_halves(first), second)

    pl.semaphore_wait(barrier, 1 + (CHIPS - 1) + 3)

    def spread(j):
        for hop in CHIP_HOPS:
            rows = table.at[j, pl.ds(own_row, OWN)]
            pltpu.make_async_remote_copy(
                src_ref=rows, dst_ref=rows, send_sem=ag_send.at[j], recv_sem=ag_recv.at[j],
                device_id=chip_peer(hop), device_id_type=MESH,
            ).start()

    def heard(j):
        for near in (above, below):
            pl.semaphore_signal(ready.at[j], inc=1, device_id=near, device_id_type=MESH)

    spread(0)
    heard(0)

    load_stations.wait()
    raw = stations_ref[...]
    spot = ((raw >> 5) & 1) * HALF + (raw >> 6) * OWN + (raw & 31)
    load_vis.wait()
    spot_f = spot.astype(F32)
    seen = vis[...].reshape(16, BASE)
    coarse = seen.astype(BF).astype(F32)
    wide[...] = jnp.zeros_like(wide)
    wide[0:16] = coarse
    wide[16:32] = seen - coarse
    wide[32:34] = spot_f

    def turn(t, _):
        at = pl.ds(pl.multiple_of(t * 128, 128), 128)
        piece = wide[:, at].T
        colb[at, :] = piece.astype(BF)
        lane = lax.broadcasted_iota(jnp.int32, (128, STATIONS), 1).astype(F32)
        per = BLOCK // 128
        for end in range(2):
            to = pl.ds(pl.multiple_of(((t // per) * 2 + end) * BLOCK + (t % per) * 128, 128), 128)
            match = piece[:, 32 + end:33 + end] == lane
            hot[to, :] = jnp.where(match, 1.0, 0.0).astype(BF)
            hot_fine[to, :] = jnp.where(match, 1.0 / FINE, 0.0).astype(F8)
        return 0

    lax.fori_loop(0, BASE // 128, turn, 0)

    def turn_t(t, _):
        at = pl.ds(pl.multiple_of(t * 32, 32), 32)
        row = (lax.broadcasted_iota(jnp.int32, (32, BASE), 0) + t * 32).astype(F32)
        hot_pt[at, :] = jnp.where(wide[32:33, :] == row, 1.0, 0.0).astype(BF)
        hot_qt[at, :] = jnp.where(wide[33:34, :] == row, 1.0, 0.0).astype(BF)
        return 0

    lax.fori_loop(0, STATIONS // 32, turn_t, 0)

    spread(1)
    out_lane = lax.broadcasted_iota(jnp.int32, (128, 256), 1)
    in_row = lax.broadcasted_iota(jnp.int32, (128, 256), 0)
    in_lane = lax.broadcasted_iota(jnp.int32, (256, 256), 0)
    out_wide = lax.broadcasted_iota(jnp.int32, (256, 256), 1)
    for j in range(PAIRS):
        want = (out_lane // 128) * 8 + 2 * j + (out_lane // 64) % 2
        hit = (in_row < 32) & (in_row % 16 == want)
        minus = jnp.where(in_lane // 64 == out_wide // 64, -1.0, 0.0).astype(BF)
        mix[j, 0:256] = minus
        mix[j, 256:512] = minus
        mix[j, 512:640] = jnp.where(hit, 1.0, 0.0).astype(BF)

    channel = lax.broadcasted_iota(jnp.int32, (1, 128), 1).astype(F32)
    rows_b = bernstein((channel + 0.5) / 128.0)
    weight_row = 4.0 * pen_row[...].astype(F32)
    lower = {}
    for r in range(TERMS):
        for q in range(r + 1):
            value = jnp.sum(weight_row * rows_b[r] * rows_b[q], axis=1, keepdims=True)
            for s in range(q):
                value = value - lower[r, s] * lower[q, s]
            lower[r, q] = jnp.sqrt(value) if r == q else value / lower[q, q]
            fac[4 * r + q:4 * r + q + 1, :] = jnp.broadcast_to(lower[r, q], (1, 128))

    load_coh.wait()
    wide_low = lax.broadcasted_iota(jnp.int32, (256, 128), 1) < 64

    def pack(t, _):
        at = pl.ds(pl.multiple_of(t * 256, 256), 256)
        for j in range(PAIRS):
            c0 = coh[2 * j, at, :].astype(F32)
            c1 = coh[2 * j + 1, at, :].astype(F32)
            packed[j, at, 0:128] = jnp.where(wide_low, c0, swap_halves(c1)).astype(BF)
            packed[j, at, 128:256] = jnp.where(wide_low, swap_halves(c0), c1).astype(BF)
        return 0

    lax.fori_loop(0, BASE // 256, pack, 0)

    def relay(j):
        got = table.at[j, pl.ds(0, (CHIPS - 1) * OWN)]
        pltpu.make_async_remote_copy(
            src_ref=got, dst_ref=got, send_sem=ag_send.at[j], recv_sem=ag_recv.at[j],
            device_id=other, device_id_type=MESH,
        ).wait_recv()
        half = table.at[j, pl.ds(pl.multiple_of(c * HALF, HALF), HALF)]
        pltpu.make_async_remote_copy(
            src_ref=half, dst_ref=half, send_sem=relay_send.at[j], recv_sem=relay_recv.at[j],
            device_id=other, device_id_type=MESH,
        ).start()

    def relay_copy(j):
        half = table.at[j, pl.ds(pl.multiple_of(c * HALF, HALF), HALF)]
        return pltpu.make_async_remote_copy(
            src_ref=half, dst_ref=half, send_sem=relay_send.at[j], recv_sem=relay_recv.at[j],
            device_id=other, device_id_type=MESH,
        )

    def core_copy(j):
        return pltpu.make_async_remote_copy(
            src_ref=sums.at[j, pl.ds(pl.multiple_of((1 - c) * HALF, HALF), HALF)],
            dst_ref=core_in.at[j], send_sem=core_send.at[j], recv_sem=core_recv.at[j],
            device_id=other, device_id_type=MESH,
        )

    def to_owners(j):
        core_copy(j).wait_recv()
        chip_sum[j] = sums[j, pl.ds(pl.multiple_of(c * HALF, HALF), HALF)] + core_in[j]
        for slot, hop in enumerate(CHIP_HOPS):
            owner = chip_at(hop)
            pltpu.make_async_remote_copy(
                src_ref=chip_sum.at[j, pl.ds(pl.multiple_of(owner * OWN, OWN), OWN)],
                dst_ref=chip_in.at[j, slot], send_sem=rs_send.at[j], recv_sem=rs_recv.at[j],
                device_id=chip_peer(hop), device_id_type=MESH,
            ).start()

    def all_in(j):
        return pltpu.make_async_remote_copy(
            src_ref=chip_in.at[j], dst_ref=chip_in.at[j], send_sem=rs_send.at[j],
            recv_sem=rs_recv.at[j], device_id=other, device_id_type=MESH,
        )


    relay(0)
    spread(2)

    def gather(b, pulled):
        at = slice(b * 2 * BLOCK, (b + 1) * 2 * BLOCK)
        pulled[...] = jnp.dot(hot[at, :], split[...], preferred_element_type=F32) + jnp.dot(
            hot_fine[at, :], fine[...], preferred_element_type=F32
        )

    def combine(j, b, pulled):
        at = slice(b * BLOCK, (b + 1) * BLOCK)
        cr = packed[j, at, 0:128].astype(F32)
        ci = packed[j, at, 128:256].astype(F32)
        nr, ni = pulled[0:BLOCK, 0:128], pulled[0:BLOCK, 128:256]
        fr, fi = pulled[BLOCK:2 * BLOCK, 0:128], pulled[BLOCK:2 * BLOCK, 128:256]
        hr = cr * fr + ci * fi
        hi = ci * fr - cr * fi
        mr = nr * hr - ni * hi
        mi = nr * hi + ni * hr
        mrh, mih = mr.astype(BF), mi.astype(BF)
        mrl = (mr - mrh.astype(F32)).astype(BF)
        mil = (mi - mih.astype(F32)).astype(BF)
        resid = jnp.dot(
            jnp.concatenate([mrh, mih, mrl, mil, colb[at, :]], 1), mix[j],
            preferred_element_type=F32,
        )
        tr = resid[:, 0:128] + mr
        ti = resid[:, 128:256] + mi
        er = cr * nr - ci * ni
        ei = cr * ni + ci * nr
        terms_p[at, 0:128] = (tr * hr + ti * hi).astype(BF)
        terms_p[at, 128:256] = (ti * hr - tr * hi).astype(BF)
        terms_p[at, 256:384] = (hr * hr + hi * hi).astype(BF)
        terms_q[at, 0:128] = (tr * er + ti * ei).astype(BF)
        terms_q[at, 128:256] = (tr * ei - ti * er).astype(BF)
        terms_q[at, 256:384] = (er * er + ei * ei).astype(BF)

    def scatter(rows, at):
        return jnp.dot(
            hot_pt[rows, at], terms_p[at, :], preferred_element_type=F32
        ) + jnp.dot(hot_qt[rows, at], terms_q[at, :], preferred_element_type=F32)

    blocks = BASE // BLOCK
    early = slice(0, BASE - BLOCK)
    late = slice(BASE - BLOCK, BASE)
    theirs = pl.ds(pl.multiple_of((1 - c) * HALF, HALF), HALF)
    mine = pl.ds(pl.multiple_of(c * HALF, HALF), HALF)

    def pair(j, _):
        relay_copy(j).wait_recv()
        whole = table[j]
        high = whole.astype(BF)
        split[...] = high
        fine[...] = ((whole - high.astype(F32)) * FINE).astype(F8)
        pulled = (pulled0, pulled1)
        gather(0, pulled[0])
        for b in range(blocks - 1):
            gather(b + 1, pulled[(b + 1) % 2])
            combine(j, b, pulled[b % 2])
            if b == 0:
                pl.when(j > 0)(lambda: to_owners(j - 1))
                pl.when(j == 0)(lambda: spread(3))

        pl.when(j + 1 < PAIRS)(lambda: relay(j + 1))
        pl.semaphore_wait(ready.at[j], 2)
        pl.when(j + 1 < PAIRS)(lambda: heard(j + 1))
        sums[j] = scatter(slice(0, STATIONS), early)
        combine(j, blocks - 1, pulled[(blocks - 1) % 2])
        sums[j, theirs, :] += scatter(theirs, late)
        core_copy(j).start()
        sums[j, mine, :] += scatter(mine, late)
        return 0

    lax.fori_loop(0, PAIRS, pair, 0)
    to_owners(PAIRS - 1)

    load_dual.wait()
    load_coeffs.wait()
    co = [coeffs_ref[t] for t in range(TERMS)]
    co_re = [jnp.where(low, v, swap_halves(v)) for v in co]
    co_im = [jnp.where(low, swap_halves(v), v) for v in co]
    half_lane = lax.broadcasted_iota(jnp.int32, (1, 128), 1)
    total = [jnp.zeros((OWN, 128), F32) for _ in range(TERMS)]
    for j in range(PAIRS):
        all_in(j).wait_recv()
        normal = chip_sum[j, pl.ds(pl.multiple_of(m * OWN, OWN), OWN)]
        for d in range(CHIPS - 1):
            normal = normal + chip_in[j, d]
        f0 = k * 8 + 2 * j
        p0 = jnp.full((1, 128), pen_smem[f0], jnp.int32)
        p1 = jnp.full((1, 128), pen_smem[f0 + 1], jnp.int32)
        w0 = 4.0 * p0.astype(F32)
        w1 = 4.0 * p1.astype(F32)
        spot0 = (jnp.full((1, 128), f0, jnp.int32).astype(F32) + 0.5) / 128.0
        spot1 = (jnp.full((1, 128), f0 + 1, jnp.int32).astype(F32) + 0.5) / 128.0
        b0, b1 = bernstein(spot0), bernstein(spot1)
        weight = jnp.where(half_lane < 64, w0, w1)
        both = [jnp.where(half_lane < 64, u, v) for u, v in zip(b0, b1)]
        d0, d1 = dual_ref[2 * j], dual_ref[2 * j + 1]
        dual_re = jnp.where(low, d0, swap_halves(d1))
        dual_im = jnp.where(low, swap_halves(d0), d1)
        prior_re = sum(both[t] * co_re[t] for t in range(TERMS))
        prior_im = sum(both[t] * co_im[t] for t in range(TERMS))
        under = normal[:, 256:384] + weight
        gain_re = (normal[:, 0:128] + weight * (prior_re - dual_re)) / under
        gain_im = (normal[:, 128:256] + weight * (prior_im - dual_im)) / under
        g0 = jnp.where(low, gain_re, swap_halves(gain_im))
        g1 = jnp.where(low, swap_halves(gain_re), gain_im)
        ng_ref[2 * j] = g0
        ng_ref[2 * j + 1] = g1
        for t in range(TERMS):
            total[t] = total[t] + (w0 * b0[t]) * (g0 + d0) + (w1 * b1[t]) * (g1 + d1)

    out_gains = pltpu.make_async_copy(ng_ref, ng_hbm, out_sem.at[0])
    out_gains.start()
    out_fac = pltpu.make_async_copy(fac, fac_hbm, out_sem.at[1])
    out_fac.start()
    for t in range(TERMS):
        mom[4 * t:4 * t + 4] = total[t].reshape(4, 8, 128)
    for slot, hop in enumerate(SUB_HOPS):
        pltpu.make_async_remote_copy(
            src_ref=mom.at[sub_at(hop)], dst_ref=mom_in.at[slot],
            send_sem=m_send, recv_sem=m_recv, device_id=sub_peer(hop), device_id_type=MESH,
        ).start()
    m_all = pltpu.make_async_remote_copy(
        src_ref=mom_in, dst_ref=mom_in, send_sem=m_send, recv_sem=m_recv,
        device_id=other, device_id_type=MESH,
    )
    m_all.wait_recv()
    tile = mom[k]
    for d in range(SUBS - 1):
        tile = tile + mom_in[d]
    mom_all[k] = tile
    for hop in SUB_HOPS:
        pltpu.make_async_remote_copy(
            src_ref=mom_all.at[k], dst_ref=mom_all.at[k],
            send_sem=r_send, recv_sem=r_recv, device_id=sub_peer(hop), device_id_type=MESH,
        ).start()
    r_all = pltpu.make_async_remote_copy(
        src_ref=mom_all.at[pl.ds(0, SUBS - 1)], dst_ref=mom_all.at[pl.ds(0, SUBS - 1)],
        send_sem=r_send, recv_sem=r_recv, device_id=other, device_id_type=MESH,
    )
    r_all.wait_recv()

    out_mom = pltpu.make_async_copy(mom_all, mom_hbm, out_sem.at[2])
    out_mom.start()

    for j in range(PAIRS):
        sent = table.at[j, pl.ds(0, (CHIPS - 1) * OWN)]
        pltpu.make_async_remote_copy(
            src_ref=sent, dst_ref=sent, send_sem=ag_send.at[j], recv_sem=ag_recv.at[j],
            device_id=other, device_id_type=MESH,
        ).wait_send()
        relay_copy(j).wait_send()
        core_copy(j).wait_send()
        all_in(j).wait_send()
    m_all.wait_send()
    r_all.wait_send()
    out_gains.wait()
    out_fac.wait()
    out_mom.wait()


def finish(ng_ref, dual_ref, mom_all, fac, ng_out, nd_ref, nc_ref):
    k = lax.axis_index("sub")
    low_of = lambda r, q: fac[4 * r + q:4 * r + q + 1, :]
    forward = []
    for r in range(TERMS):
        value = mom_all[4 * r:4 * r + 4].reshape(OWN, 128)
        for q in range(r):
            value = value - low_of(r, q) * forward[q]
        forward.append(value / low_of(r, r))
    back = [None] * TERMS
    for r in range(TERMS - 1, -1, -1):
        value = forward[r]
        for q in range(r + 1, TERMS):
            value = value - low_of(q, r) * back[q]
        back[r] = value / low_of(r, r)
        nc_ref[r] = back[r]
    for f in range(2 * PAIRS):
        spot = (jnp.full((1, 128), k * 8 + f, jnp.int32).astype(F32) + 0.5) / 128.0
        basis = bernstein(spot)
        agreed = sum(basis[t] * back[t] for t in range(TERMS))
        gain = ng_ref[f]
        ng_out[f] = gain
        nd_ref[f] = dual_ref[f] + gain - agreed


def step(coherency, visibility, stations, gains, dual, coeffs, penalty):
    vmem = pl.BlockSpec(memory_space=pltpu.VMEM)
    hbm = pl.BlockSpec(memory_space=pl.ANY)
    dma = pltpu.SemaphoreType.DMA
    gained, moments, factor = pl.pallas_call(
        kernel,
        out_shape=(
            jax.ShapeDtypeStruct(gains.shape, F32),
            jax.ShapeDtypeStruct((SUBS, 8, 128), F32),
            jax.ShapeDtypeStruct((16, 128), F32),
        ),
        in_specs=[hbm, hbm, hbm, hbm, hbm, hbm, vmem, pl.BlockSpec(memory_space=pltpu.SMEM)],
        out_specs=(hbm, hbm, hbm),
        scratch_shapes=[
            pltpu.VMEM((8, BASE, 128), BF),
            pltpu.VMEM((PAIRS, BASE, 256), BF),
            pltpu.VMEM((2, 8, BASE), F32),
            pltpu.VMEM((8, OWN, 128), F32),
            pltpu.VMEM((8, OWN, 128), F32),
            pltpu.VMEM((TERMS, OWN, 128), F32),
            pltpu.VMEM((2, BASE), jnp.int32),
            pltpu.VMEM((8, OWN, 128), F32),
            pltpu.VMEM((128, BASE), F32),
            pltpu.VMEM((BASE, 128), BF),
            pltpu.VMEM((2 * BASE, STATIONS), BF),
            pltpu.VMEM((STATIONS, BASE), BF),
            pltpu.VMEM((STATIONS, BASE), BF),
            pltpu.VMEM((PAIRS, 640, 256), BF),
            pltpu.VMEM((PAIRS, STATIONS, 256), F32),
            pltpu.VMEM((STATIONS, 256), BF),
            pltpu.VMEM((STATIONS, 256), F8),
            pltpu.VMEM((2 * BASE, STATIONS), F8),
            pltpu.VMEM((2 * BLOCK, 256), F32),
            pltpu.VMEM((2 * BLOCK, 256), F32),
            pltpu.VMEM((BASE, 384), BF),
            pltpu.VMEM((BASE, 384), BF),
            pltpu.VMEM((PAIRS, STATIONS, 384), F32),
            pltpu.VMEM((PAIRS, HALF, 384), F32),
            pltpu.VMEM((PAIRS, HALF, 384), F32),
            pltpu.VMEM((PAIRS, CHIPS - 1, OWN, 384), F32),
            pltpu.VMEM((SUBS, 8, 128), F32),
            pltpu.VMEM((SUBS - 1, 8, 128), F32),
            pltpu.VMEM((SUBS, 8, 128), F32),
            pltpu.VMEM((16, 128), F32),
            pltpu.SemaphoreType.REGULAR((PAIRS,)), dma((6,)), dma((3,)),
            dma((PAIRS,)), dma((PAIRS,)),
            dma((PAIRS,)), dma((PAIRS,)),
            dma((PAIRS,)), dma((PAIRS,)),
            dma((PAIRS,)), dma((PAIRS,)),
            dma(()), dma(()), dma(()), dma(()),
        ],
        compiler_params=pltpu.CompilerParams(
            collective_id=0, has_side_effects=True, vmem_limit_bytes=56 * 1024 * 1024
        ),
    )(coherency, visibility, gains, dual, coeffs, stations, penalty.reshape(1, 128), penalty)
    return pl.pallas_call(
        finish,
        out_shape=(
            jax.ShapeDtypeStruct(gains.shape, F32),
            jax.ShapeDtypeStruct(gains.shape, F32),
            jax.ShapeDtypeStruct(coeffs.shape, F32),
        ),
        in_specs=[vmem] * 4,
        out_specs=(vmem,) * 3,
    )(gained, dual, moments, factor)


def solution(mesh):
    placed = (
        P("sub", "bl", None),
        P(None, "sub", "bl"),
        P(None, "bl"),
        P("sub", "bl", None),
        P("sub", "bl", None),
        P(None, "bl", None),
        P(),
    )
    return jax.shard_map(
        step,
        mesh=mesh,
        in_specs=placed,
        out_specs=(P("sub", "bl", None), P("sub", "bl", None), P(None, "bl", None)),
        check_vma=False,
    )
```

```python
import functools
import math

import jax
import jax.numpy as jnp
from jax import lax
from jax.experimental import pallas as pl
from jax.experimental.pallas import tpu as pltpu
from jax.sharding import PartitionSpec as P

MESH = pl.DeviceIdType.MESH
BF = jnp.bfloat16
F32 = jnp.float32
F8 = jnp.float8_e5m2
FINE = 256.0
PAIRS = 4
STATIONS = 512
HALF = 256
OWN = 32
BASE = 2048
CHIPS = 8
SUBS = 16
TERMS = 4
BLOCK = 512
CHIP_HOPS = ((2, 1), (2, 0), (1, 1), (3, 1), (0, 1), (1, 0), (3, 0))
SUB_HOPS = (
    (1, 4), (0, 4), (1, 3), (1, 5), (0, 3), (0, 5), (1, 2), (1, 6),
    (0, 2), (0, 6), (1, 1), (1, 7), (0, 1), (0, 7), (1, 0),
)


def bernstein(position):
    degree = TERMS - 1
    rest = 1.0 - position
    out = []
    for order in range(TERMS):
        value = jnp.full_like(position, float(math.comb(degree, order)))
        for _ in range(order):
            value = value * position
        for _ in range(degree - order):
            value = value * rest
        out.append(value)
    return out


def swap_halves(value):
    return pltpu.roll(value, 64, 1)


def kernel(
    coh_hbm, vis_hbm, gains_hbm, dual_hbm, coeffs_hbm, stations_hbm, pen_row, pen_smem,
    ng_hbm, mom_hbm, fac_hbm,
    coh, packed, vis, gains_ref, dual_ref, coeffs_ref, stations_ref, ng_ref,
    wide, colb, hot, hot_pt, hot_qt, mix,
    table, split, fine, hot_fine, pulled0, pulled1, terms_p, terms_q, sums, core_in, chip_sum, chip_in,
    mom, mom_in, mom_all, fac,
    ready, load_sem, out_sem, ag_send, ag_recv, relay_send, relay_recv, core_send, core_recv,
    rs_send, rs_recv, m_send, m_recv, r_send, r_recv,
):
    k = lax.axis_index("sub")
    i = lax.axis_index("bl")
    m = i // 2
    c = i % 2
    other = (k, m * 2 + (1 - c))

    def chip_at(hop):
        return lax.rem(m // 2 + hop[0], 4) * 2 + lax.rem(m + hop[1], 2)

    def chip_peer(hop):
        return (k, chip_at(hop) * 2 + c)

    def sub_at(hop):
        return lax.rem(k // 8 + hop[0], 2) * 8 + lax.rem(k + hop[1], 8)

    def sub_peer(hop):
        return (sub_at(hop), i)

    barrier = pltpu.get_barrier_semaphore()
    pl.semaphore_signal(barrier, inc=1, device_id=other, device_id_type=MESH)
    for hop in CHIP_HOPS:
        pl.semaphore_signal(barrier, inc=1, device_id=chip_peer(hop), device_id_type=MESH)
    above, below = sub_peer((0, 1)), sub_peer((0, 7))
    for near in (above, below, sub_peer((1, 0))):
        pl.semaphore_signal(barrier, inc=1, device_id=near, device_id_type=MESH)

    load_gains = pltpu.make_async_copy(gains_hbm, gains_ref, load_sem.at[2])
    load_gains.start()
    load_stations = pltpu.make_async_copy(stations_hbm, stations_ref, load_sem.at[3])
    load_stations.start()
    load_vis = pltpu.make_async_copy(vis_hbm, vis, load_sem.at[0])
    load_vis.start()
    load_coh = pltpu.make_async_copy(coh_hbm, coh, load_sem.at[1])
    load_coh.start()
    load_dual = pltpu.make_async_copy(dual_hbm, dual_ref, load_sem.at[4])
    load_dual.start()
    load_coeffs = pltpu.make_async_copy(coeffs_hbm, coeffs_ref, load_sem.at[5])
    load_coeffs.start()

    low = lax.broadcasted_iota(jnp.int32, (OWN, 128), 1) < 64
    load_gains.wait()
    own_row = pl.multiple_of(c * HALF + m * OWN, OWN)
    for j in range(PAIRS):
        first, second = gains_ref[2 * j], gains_ref[2 * j + 1]
        table[j, pl.ds(own_row, OWN), 0:128] = jnp.where(low, first, swap_halves(second))
        table[j, pl.ds(own_row, OWN), 128:256] = jnp.where(low, swap_halves(first), second)

    pl.semaphore_wait(barrier, 1 + (CHIPS - 1) + 3)

    def spread(j):
        for hop in CHIP_HOPS:
            rows = table.at[j, pl.ds(own_row, OWN)]
            pltpu.make_async_remote_copy(
                src_ref=rows, dst_ref=rows, send_sem=ag_send.at[j], recv_sem=ag_recv.at[j],
                device_id=chip_peer(hop), device_id_type=MESH,
            ).start()

    def heard(j):
        for near in (above, below):
            pl.semaphore_signal(ready.at[j], inc=1, device_id=near, device_id_type=MESH)

    spread(0)
    heard(0)

    load_stations.wait()
    raw = stations_ref[...]
    spot = ((raw >> 5) & 1) * HALF + (raw >> 6) * OWN + (raw & 31)
    load_vis.wait()
    spot_f = spot.astype(F32)
    seen = vis[...].reshape(16, BASE)
    coarse = seen.astype(BF).astype(F32)
    wide[...] = jnp.zeros_like(wide)
    wide[0:16] = coarse
    wide[16:32] = seen - coarse
    wide[32:34] = spot_f

    def turn(t, _):
        at = pl.ds(pl.multiple_of(t * 128, 128), 128)
        piece = wide[:, at].T
        colb[at, :] = piece.astype(BF)
        lane = lax.broadcasted_iota(jnp.int32, (128, STATIONS), 1).astype(F32)
        per = BLOCK // 128
        for end in range(2):
            to = pl.ds(pl.multiple_of(((t // per) * 2 + end) * BLOCK + (t % per) * 128, 128), 128)
            match = piece[:, 32 + end:33 + end] == lane
            hot[to, :] = jnp.where(match, 1.0, 0.0).astype(BF)
            hot_fine[to, :] = jnp.where(match, 1.0 / FINE, 0.0).astype(F8)
        return 0

    lax.fori_loop(0, BASE // 128, turn, 0)

    def turn_t(t, _):
        at = pl.ds(pl.multiple_of(t * 32, 32), 32)
        row = (lax.broadcasted_iota(jnp.int32, (32, BASE), 0) + t * 32).astype(F32)
        hot_pt[at, :] = jnp.where(wide[32:33, :] == row, 1.0, 0.0).astype(BF)
        hot_qt[at, :] = jnp.where(wide[33:34, :] == row, 1.0, 0.0).astype(BF)
        return 0

    lax.fori_loop(0, STATIONS // 32, turn_t, 0)

    spread(1)
    out_lane = lax.broadcasted_iota(jnp.int32, (128, 256), 1)
    in_row = lax.broadcasted_iota(jnp.int32, (128, 256), 0)
    in_lane = lax.broadcasted_iota(jnp.int32, (256, 256), 0)
    out_wide = lax.broadcasted_iota(jnp.int32, (256, 256), 1)
    for j in range(PAIRS):
        want = (out_lane // 128) * 8 + 2 * j + (out_lane // 64) % 2
        hit = (in_row < 32) & (in_row % 16 == want)
        minus = jnp.where(in_lane // 64 == out_wide // 64, -1.0, 0.0).astype(BF)
        mix[j, 0:256] = minus
        mix[j, 256:512] = minus
        mix[j, 512:640] = jnp.where(hit, 1.0, 0.0).astype(BF)

    channel = lax.broadcasted_iota(jnp.int32, (1, 128), 1).astype(F32)
    rows_b = bernstein((channel + 0.5) / 128.0)
    weight_row = 4.0 * pen_row[...].astype(F32)
    lower = {}
    for r in range(TERMS):
        for q in range(r + 1):
            value = jnp.sum(weight_row * rows_b[r] * rows_b[q], axis=1, keepdims=True)
            for s in range(q):
                value = value - lower[r, s] * lower[q, s]
            lower[r, q] = jnp.sqrt(value) if r == q else value / lower[q, q]
            fac[4 * r + q:4 * r + q + 1, :] = jnp.broadcast_to(lower[r, q], (1, 128))

    load_coh.wait()
    wide_low = lax.broadcasted_iota(jnp.int32, (256, 128), 1) < 64

    def pack(t, _):
        at = pl.ds(pl.multiple_of(t * 256, 256), 256)
        for j in range(PAIRS):
            c0 = coh[2 * j, at, :].astype(F32)
            c1 = coh[2 * j + 1, at, :].astype(F32)
            packed[j, at, 0:128] = jnp.where(wide_low, c0, swap_halves(c1)).astype(BF)
            packed[j, at, 128:256] = jnp.where(wide_low, swap_halves(c0), c1).astype(BF)
        return 0

    lax.fori_loop(0, BASE // 256, pack, 0)

    def relay(j):
        got = table.at[j, pl.ds(0, (CHIPS - 1) * OWN)]
        pltpu.make_async_remote_copy(
            src_ref=got, dst_ref=got, send_sem=ag_send.at[j], recv_sem=ag_recv.at[j],
            device_id=other, device_id_type=MESH,
        ).wait_recv()
        half = table.at[j, pl.ds(pl.multiple_of(c * HALF, HALF), HALF)]
        pltpu.make_async_remote_copy(
            src_ref=half, dst_ref=half, send_sem=relay_send.at[j], recv_sem=relay_recv.at[j],
            device_id=other, device_id_type=MESH,
        ).start()

    def relay_copy(j):
        half = table.at[j, pl.ds(pl.multiple_of(c * HALF, HALF), HALF)]
        return pltpu.make_async_remote_copy(
            src_ref=half, dst_ref=half, send_sem=relay_send.at[j], recv_sem=relay_recv.at[j],
            device_id=other, device_id_type=MESH,
        )

    def core_copy(j):
        return pltpu.make_async_remote_copy(
            src_ref=sums.at[j, pl.ds(pl.multiple_of((1 - c) * HALF, HALF), HALF)],
            dst_ref=core_in.at[j], send_sem=core_send.at[j], recv_sem=core_recv.at[j],
            device_id=other, device_id_type=MESH,
        )

    def to_owners(j):
        core_copy(j).wait_recv()
        for slot, hop in enumerate(CHIP_HOPS + ((0, 0),)):
            owner = chip_at(hop)
            rows = pl.ds(pl.multiple_of(owner * OWN, OWN), OWN)
            ours = pl.ds(pl.multiple_of(c * HALF + owner * OWN, OWN), OWN)
            chip_sum[j, rows] = sums[j, ours] + core_in[j, rows]
            if hop == (0, 0):
                continue
            pltpu.make_async_remote_copy(
                src_ref=chip_sum.at[j, pl.ds(pl.multiple_of(owner * OWN, OWN), OWN)],
                dst_ref=chip_in.at[j, slot], send_sem=rs_send.at[j], recv_sem=rs_recv.at[j],
                device_id=chip_peer(hop), device_id_type=MESH,
            ).start()

    def all_in(j):
        return pltpu.make_async_remote_copy(
            src_ref=chip_in.at[j], dst_ref=chip_in.at[j], send_sem=rs_send.at[j],
            recv_sem=rs_recv.at[j], device_id=other, device_id_type=MESH,
        )


    relay(0)
    spread(2)

    def gather(b, pulled):
        at = slice(b * 2 * BLOCK, (b + 1) * 2 * BLOCK)
        pulled[...] = jnp.dot(hot[at, :], split[...], preferred_element_type=F32) + jnp.dot(
            hot_fine[at, :], fine[...], preferred_element_type=F32
        )

    def combine(j, b, pulled):
        at = slice(b * BLOCK, (b + 1) * BLOCK)
        cr = packed[j, at, 0:128].astype(F32)
        ci = packed[j, at, 128:256].astype(F32)
        nr, ni = pulled[0:BLOCK, 0:128], pulled[0:BLOCK, 128:256]
        fr, fi = pulled[BLOCK:2 * BLOCK, 0:128], pulled[BLOCK:2 * BLOCK, 128:256]
        hr = cr * fr + ci * fi
        hi = ci * fr - cr * fi
        mr = nr * hr - ni * hi
        mi = nr * hi + ni * hr
        mrh, mih = mr.astype(BF), mi.astype(BF)
        mrl = (mr - mrh.astype(F32)).astype(BF)
        mil = (mi - mih.astype(F32)).astype(BF)
        resid = jnp.dot(
            jnp.concatenate([mrh, mih, mrl, mil, colb[at, :]], 1), mix[j],
            preferred_element_type=F32,
        )
        tr = resid[:, 0:128] + mr
        ti = resid[:, 128:256] + mi
        er = cr * nr - ci * ni
        ei = cr * ni + ci * nr
        terms_p[at, 0:128] = (tr * hr + ti * hi).astype(BF)
        terms_p[at, 128:256] = (ti * hr - tr * hi).astype(BF)
        terms_p[at, 256:384] = (hr * hr + hi * hi).astype(BF)
        terms_q[at, 0:128] = (tr * er + ti * ei).astype(BF)
        terms_q[at, 128:256] = (tr * ei - ti * er).astype(BF)
        terms_q[at, 256:384] = (er * er + ei * ei).astype(BF)

    def scatter(rows, at):
        return jnp.dot(
            hot_pt[rows, at], terms_p[at, :], preferred_element_type=F32
        ) + jnp.dot(hot_qt[rows, at], terms_q[at, :], preferred_element_type=F32)

    blocks = BASE // BLOCK
    early = slice(0, BASE - BLOCK)
    late = slice(BASE - BLOCK, BASE)
    theirs = pl.ds(pl.multiple_of((1 - c) * HALF, HALF), HALF)
    mine = pl.ds(pl.multiple_of(c * HALF, HALF), HALF)

    def pair(j, _):
        relay_copy(j).wait_recv()
        whole = table[j]
        high = whole.astype(BF)
        split[...] = high
        fine[...] = ((whole - high.astype(F32)) * FINE).astype(F8)
        pulled = (pulled0, pulled1)
        gather(0, pulled[0])
        for b in range(blocks - 1):
            gather(b + 1, pulled[(b + 1) % 2])
            combine(j, b, pulled[b % 2])
            if b == 0:
                pl.when(j > 0)(lambda: to_owners(j - 1))
                pl.when(j == 0)(lambda: spread(3))

        pl.when(j + 1 < PAIRS)(lambda: relay(j + 1))
        pl.semaphore_wait(ready.at[j], 2)
        pl.when(j + 1 < PAIRS)(lambda: heard(j + 1))
        sums[j] = scatter(slice(0, STATIONS), early)
        combine(j, blocks - 1, pulled[(blocks - 1) % 2])
        sums[j, theirs, :] += scatter(theirs, late)
        core_copy(j).start()
        sums[j, mine, :] += scatter(mine, late)
        return 0

    lax.fori_loop(0, PAIRS, pair, 0)
    to_owners(PAIRS - 1)

    load_dual.wait()
    load_coeffs.wait()
    co = [coeffs_ref[t] for t in range(TERMS)]
    co_re = [jnp.where(low, v, swap_halves(v)) for v in co]
    co_im = [jnp.where(low, swap_halves(v), v) for v in co]
    half_lane = lax.broadcasted_iota(jnp.int32, (1, 128), 1)
    total = [jnp.zeros((OWN, 128), F32) for _ in range(TERMS)]
    for j in range(PAIRS):
        all_in(j).wait_recv()
        normal = chip_sum[j, pl.ds(pl.multiple_of(m * OWN, OWN), OWN)]
        for d in range(CHIPS - 1):
            normal = normal + chip_in[j, d]
        f0 = k * 8 + 2 * j
        p0 = jnp.full((1, 128), pen_smem[f0], jnp.int32)
        p1 = jnp.full((1, 128), pen_smem[f0 + 1], jnp.int32)
        w0 = 4.0 * p0.astype(F32)
        w1 = 4.0 * p1.astype(F32)
        spot0 = (jnp.full((1, 128), f0, jnp.int32).astype(F32) + 0.5) / 128.0
        spot1 = (jnp.full((1, 128), f0 + 1, jnp.int32).astype(F32) + 0.5) / 128.0
        b0, b1 = bernstein(spot0), bernstein(spot1)
        weight = jnp.where(half_lane < 64, w0, w1)
        both = [jnp.where(half_lane < 64, u, v) for u, v in zip(b0, b1)]
        d0, d1 = dual_ref[2 * j], dual_ref[2 * j + 1]
        dual_re = jnp.where(low, d0, swap_halves(d1))
        dual_im = jnp.where(low, swap_halves(d0), d1)
        prior_re = sum(both[t] * co_re[t] for t in range(TERMS))
        prior_im = sum(both[t] * co_im[t] for t in range(TERMS))
        under = normal[:, 256:384] + weight
        gain_re = (normal[:, 0:128] + weight * (prior_re - dual_re)) / under
        gain_im = (normal[:, 128:256] + weight * (prior_im - dual_im)) / under
        g0 = jnp.where(low, gain_re, swap_halves(gain_im))
        g1 = jnp.where(low, swap_halves(gain_re), gain_im)
        ng_ref[2 * j] = g0
        ng_ref[2 * j + 1] = g1
        for t in range(TERMS):
            total[t] = total[t] + (w0 * b0[t]) * (g0 + d0) + (w1 * b1[t]) * (g1 + d1)

    out_gains = pltpu.make_async_copy(ng_ref, ng_hbm, out_sem.at[0])
    out_gains.start()
    out_fac = pltpu.make_async_copy(fac, fac_hbm, out_sem.at[1])
    out_fac.start()
    for t in range(TERMS):
        mom[4 * t:4 * t + 4] = total[t].reshape(4, 8, 128)
    for slot, hop in enumerate(SUB_HOPS):
        pltpu.make_async_remote_copy(
            src_ref=mom.at[sub_at(hop)], dst_ref=mom_in.at[slot],
            send_sem=m_send, recv_sem=m_recv, device_id=sub_peer(hop), device_id_type=MESH,
        ).start()
    m_all = pltpu.make_async_remote_copy(
        src_ref=mom_in, dst_ref=mom_in, send_sem=m_send, recv_sem=m_recv,
        device_id=other, device_id_type=MESH,
    )
    m_all.wait_recv()
    tile = mom[k]
    for d in range(SUBS - 1):
        tile = tile + mom_in[d]
    mom_all[k] = tile
    for hop in SUB_HOPS:
        pltpu.make_async_remote_copy(
            src_ref=mom_all.at[k], dst_ref=mom_all.at[k],
            send_sem=r_send, recv_sem=r_recv, device_id=sub_peer(hop), device_id_type=MESH,
        ).start()
    r_all = pltpu.make_async_remote_copy(
        src_ref=mom_all.at[pl.ds(0, SUBS - 1)], dst_ref=mom_all.at[pl.ds(0, SUBS - 1)],
        send_sem=r_send, recv_sem=r_recv, device_id=other, device_id_type=MESH,
    )
    r_all.wait_recv()

    out_mom = pltpu.make_async_copy(mom_all, mom_hbm, out_sem.at[2])
    out_mom.start()

    for j in range(PAIRS):
        sent = table.at[j, pl.ds(0, (CHIPS - 1) * OWN)]
        pltpu.make_async_remote_copy(
            src_ref=sent, dst_ref=sent, send_sem=ag_send.at[j], recv_sem=ag_recv.at[j],
            device_id=other, device_id_type=MESH,
        ).wait_send()
        relay_copy(j).wait_send()
        core_copy(j).wait_send()
        all_in(j).wait_send()
    m_all.wait_send()
    r_all.wait_send()
    out_gains.wait()
    out_fac.wait()
    out_mom.wait()


def finish(ng_ref, dual_ref, mom_all, fac, ng_out, nd_ref, nc_ref):
    k = lax.axis_index("sub")
    low_of = lambda r, q: fac[4 * r + q:4 * r + q + 1, :]
    forward = []
    for r in range(TERMS):
        value = mom_all[4 * r:4 * r + 4].reshape(OWN, 128)
        for q in range(r):
            value = value - low_of(r, q) * forward[q]
        forward.append(value / low_of(r, r))
    back = [None] * TERMS
    for r in range(TERMS - 1, -1, -1):
        value = forward[r]
        for q in range(r + 1, TERMS):
            value = value - low_of(q, r) * back[q]
        back[r] = value / low_of(r, r)
        nc_ref[r] = back[r]
    for f in range(2 * PAIRS):
        spot = (jnp.full((1, 128), k * 8 + f, jnp.int32).astype(F32) + 0.5) / 128.0
        basis = bernstein(spot)
        agreed = sum(basis[t] * back[t] for t in range(TERMS))
        gain = ng_ref[f]
        ng_out[f] = gain
        nd_ref[f] = dual_ref[f] + gain - agreed


def step(coherency, visibility, stations, gains, dual, coeffs, penalty):
    vmem = pl.BlockSpec(memory_space=pltpu.VMEM)
    hbm = pl.BlockSpec(memory_space=pl.ANY)
    dma = pltpu.SemaphoreType.DMA
    gained, moments, factor = pl.pallas_call(
        kernel,
        out_shape=(
            jax.ShapeDtypeStruct(gains.shape, F32),
            jax.ShapeDtypeStruct((SUBS, 8, 128), F32),
            jax.ShapeDtypeStruct((16, 128), F32),
        ),
        in_specs=[hbm, hbm, hbm, hbm, hbm, hbm, vmem, pl.BlockSpec(memory_space=pltpu.SMEM)],
        out_specs=(hbm, hbm, hbm),
        scratch_shapes=[
            pltpu.VMEM((8, BASE, 128), BF),
            pltpu.VMEM((PAIRS, BASE, 256), BF),
            pltpu.VMEM((2, 8, BASE), F32),
            pltpu.VMEM((8, OWN, 128), F32),
            pltpu.VMEM((8, OWN, 128), F32),
            pltpu.VMEM((TERMS, OWN, 128), F32),
            pltpu.VMEM((2, BASE), jnp.int32),
            pltpu.VMEM((8, OWN, 128), F32),
            pltpu.VMEM((128, BASE), F32),
            pltpu.VMEM((BASE, 128), BF),
            pltpu.VMEM((2 * BASE, STATIONS), BF),
            pltpu.VMEM((STATIONS, BASE), BF),
            pltpu.VMEM((STATIONS, BASE), BF),
            pltpu.VMEM((PAIRS, 640, 256), BF),
            pltpu.VMEM((PAIRS, STATIONS, 256), F32),
            pltpu.VMEM((STATIONS, 256), BF),
            pltpu.VMEM((STATIONS, 256), F8),
            pltpu.VMEM((2 * BASE, STATIONS), F8),
            pltpu.VMEM((2 * BLOCK, 256), F32),
            pltpu.VMEM((2 * BLOCK, 256), F32),
            pltpu.VMEM((BASE, 384), BF),
            pltpu.VMEM((BASE, 384), BF),
            pltpu.VMEM((PAIRS, STATIONS, 384), F32),
            pltpu.VMEM((PAIRS, HALF, 384), F32),
            pltpu.VMEM((PAIRS, HALF, 384), F32),
            pltpu.VMEM((PAIRS, CHIPS - 1, OWN, 384), F32),
            pltpu.VMEM((SUBS, 8, 128), F32),
            pltpu.VMEM((SUBS - 1, 8, 128), F32),
            pltpu.VMEM((SUBS, 8, 128), F32),
            pltpu.VMEM((16, 128), F32),
            pltpu.SemaphoreType.REGULAR((PAIRS,)), dma((6,)), dma((3,)),
            dma((PAIRS,)), dma((PAIRS,)),
            dma((PAIRS,)), dma((PAIRS,)),
            dma((PAIRS,)), dma((PAIRS,)),
            dma((PAIRS,)), dma((PAIRS,)),
            dma(()), dma(()), dma(()), dma(()),
        ],
        compiler_params=pltpu.CompilerParams(
            collective_id=0, has_side_effects=True, vmem_limit_bytes=56 * 1024 * 1024
        ),
    )(coherency, visibility, gains, dual, coeffs, stations, penalty.reshape(1, 128), penalty)
    return pl.pallas_call(
        finish,
        out_shape=(
            jax.ShapeDtypeStruct(gains.shape, F32),
            jax.ShapeDtypeStruct(gains.shape, F32),
            jax.ShapeDtypeStruct(coeffs.shape, F32),
        ),
        in_specs=[vmem] * 4,
        out_specs=(vmem,) * 3,
    )(gained, dual, moments, factor)


def solution(mesh):
    placed = (
        P("sub", "bl", None),
        P(None, "sub", "bl"),
        P(None, "bl"),
        P("sub", "bl", None),
        P("sub", "bl", None),
        P(None, "bl", None),
        P(),
    )
    return jax.shard_map(
        step,
        mesh=mesh,
        in_specs=placed,
        out_specs=(P("sub", "bl", None), P("sub", "bl", None), P(None, "bl", None)),
        check_vma=False,
    )
```
